256 devices in a mesh: ctx: 64 (over z, x, core), head: 4 (over y).
Axes of the slice: x: 4, y: 4, z: 8, core: 2. Of those that a mesh axis runs over, the one named last changes fastest.
Arguments:
- query: bfloat16 [32768, 4096], P('ctx', 'head'), may hold values from -40 to 40
- keys: bfloat16 [32768, 4096], P('ctx', 'head'), may hold values from -6 to 6
- values: bfloat16 [32768, 4096], P('ctx', 'head'), may hold values from -6 to 6
- gain: float32 [4096], P('head'), may hold values from 0.5 to 2
- cotangent: bfloat16 [32768, 4096], P('ctx', 'head'), may hold values from -6 to 6
Outputs:
- attended: bfloat16 [32768, 4096], P('ctx', 'head')
- grad_query: bfloat16 [32768, 4096], P('ctx', 'head')
- grad_keys: bfloat16 [32768, 4096], P('ctx', 'head')
- grad_values: bfloat16 [32768, 4096], P('ctx', 'head')
The draws below stay inside these ranges and needn't reach their ends.
All inputs are finite; a program needn't handle non-finite values.
Results may differ from the reference program's by a relative error of at most 0.006.
Values sent between devices are 32-bit elements; how exact they have to be, the bound alone decides.
No kernel may reach another device: no remote copies, remote signals or barrier semaphores. Data moves between devices by JAX's collectives and lax.ppermute only.
A program may use at most 128 MiB of HBM per device.

```python
import math
import jax
import jax.numpy as jnp
from jax import lax

HEADS = 32
HEAD_DIM = 128
TOK_DEV = 512
TOKENS = 32768
N_CTX = 64


def draw_query(key, part):
    key = jax.random.fold_in(key, 11)
    head_key, entry_key = jax.random.split(key)
    jitter = jax.random.uniform(head_key, (HEADS,), jnp.float32)
    ladder = jnp.arange(HEADS).astype(jnp.float32)
    head_scale = jnp.exp(math.log(10.0) * (ladder + jitter) / HEADS)
    entries = jax.random.truncated_normal(entry_key, -4.0, 4.0, (TOKENS, HEADS, HEAD_DIM), jnp.float32)
    drawn = entries * head_scale[None, :, None]
    return drawn.reshape(TOKENS, HEADS * HEAD_DIM).astype(jnp.bfloat16)


def steps_of(key, extent, shards, smallest, high):
    factor_of = 1.0
    for dim, shards_of in shards:
        draws = jax.random.uniform(jax.random.fold_in(jax.random.fold_in(key, 6), dim), (shards_of,), jnp.float32, smallest / len(shards), high / len(shards))
        factor_of = factor_of * jnp.repeat(jnp.exp(draws), extent[dim] // shards_of).reshape((-1,) + (1,) * (len(extent) - 1 - dim))
    return factor_of


def bell_draw(stream_key, extent, spread, bound, pieces=(), dtype=jnp.bfloat16):
    values = spread * jax.random.normal(stream_key, extent, jnp.float32)
    if pieces:
        values = values * steps_of(stream_key, extent, pieces, -0.22, 0.18)
    return jnp.clip(values, -bound, bound).astype(dtype)


def setup_inputs(seed: int = 0) -> dict:
    splits = jax.random.split(jax.random.key(seed), 6)
    return {
        "query": draw_query(jax.random.fold_in(splits[5], 71), 0),
        "keys": bell_draw(splits[1], (TOKENS, HEADS * HEAD_DIM), 1.0, 6.0, ((0, 64), (1, 4))),
        "values": bell_draw(splits[2], (TOKENS, HEADS * HEAD_DIM), 1.0, 6.0, ((0, 64), (1, 4))),
        "gain": jnp.clip(jnp.exp(math.log(2.0) - 1.3862944 * jax.random.uniform(splits[3], (HEADS * HEAD_DIM,), jnp.float32) ** steps_of(splits[3], (HEADS * HEAD_DIM,), ((0, 4),), -0.2, 0.2)), 0.5, 2.0),
        "cotangent": bell_draw(splits[4], (TOKENS, HEADS * HEAD_DIM), 1.0, 6.0, ((0, 64), (1, 4))),
    }


EPSILON = 1e-05

def as_float(array):
    return array.astype(jnp.float32)

def causal_mask(length):
    rows = lax.broadcasted_iota(jnp.int32, (length, length), 0)
    cols = lax.broadcasted_iota(jnp.int32, (length, length), 1)
    return cols <= rows

def reference(query, keys, values, gain, cotangent):
    layout = (N_CTX, TOK_DEV, HEADS, HEAD_DIM)
    width_all = HEADS * HEAD_DIM
    q_blocks = query.reshape(layout)
    k_blocks = keys.reshape(layout)
    v_blocks = values.reshape(layout)
    c_blocks = cotangent.reshape((N_CTX, TOK_DEV, width_all))
    causal = causal_mask(TOK_DEV)

    def local_state(pair):
        return jnp.einsum('thd,the->hde', as_float(pair[0]), as_float(pair[1]))
    states = lax.map(local_state, (k_blocks, v_blocks))
    zeros = jnp.zeros((1, HEADS, HEAD_DIM, HEAD_DIM), jnp.float32)
    before = jnp.concatenate([zeros, jnp.cumsum(states, axis=0)[:-1]], axis=0)
    state_round = before.astype(jnp.bfloat16)

    def forward_block(items):
        q_block, k_block, v_block, s_block, c_block = items
        scores = jnp.einsum('thd,shd->hts', as_float(q_block), as_float(k_block))
        weights = jnp.where(causal[None], scores, 0.0).astype(jnp.bfloat16)
        mixture = jnp.einsum('hts,she->the', as_float(weights), as_float(v_block))
        mixture = mixture + jnp.einsum('thd,hde->the', as_float(q_block), as_float(s_block))
        flattened = mixture.reshape(TOK_DEV, width_all)
        squares = lax.optimization_barrier(jnp.sum(flattened * flattened, axis=1))
        inverse = lax.rsqrt(squares / width_all + EPSILON)
        attended = (flattened * inverse[:, None] * gain[None, :]).astype(jnp.bfloat16)
        scaled = as_float(c_block) * gain[None, :]
        products = lax.optimization_barrier(jnp.sum(scaled * flattened, axis=1))
        grad_flat = inverse[:, None] * scaled - flattened * (inverse ** 3 * products / width_all)[:, None]
        grad_mixture = grad_flat.astype(jnp.bfloat16).reshape(TOK_DEV, HEADS, HEAD_DIM)
        back_state = jnp.einsum('thd,the->hde', as_float(q_block), as_float(grad_mixture))
        return (attended, grad_mixture, back_state)
    attended, grad_mixture, back_states = lax.map(forward_block, (q_blocks, k_blocks, v_blocks, state_round, c_blocks))
    inclusive = jnp.cumsum(back_states[::-1], axis=0)[::-1]
    after = jnp.concatenate([inclusive[1:], zeros], axis=0)
    after_round = after.astype(jnp.bfloat16)

    def backward_block(items):
        q_block, k_block, v_block, s_block, r_block, g_block = items
        scores = jnp.einsum('thd,shd->hts', as_float(q_block), as_float(k_block))
        weights = jnp.where(causal[None], scores, 0.0).astype(jnp.bfloat16)
        grad_scores = jnp.einsum('the,she->hts', as_float(g_block), as_float(v_block))
        grad_weights = jnp.where(causal[None], grad_scores, 0.0).astype(jnp.bfloat16)
        grad_q = jnp.einsum('hts,shd->thd', as_float(grad_weights), as_float(k_block))
        grad_q = grad_q + jnp.einsum('the,hde->thd', as_float(g_block), as_float(s_block))
        grad_k = jnp.einsum('hts,thd->shd', as_float(grad_weights), as_float(q_block))
        grad_k = grad_k + jnp.einsum('she,hde->shd', as_float(v_block), as_float(r_block))
        grad_v = jnp.einsum('hts,the->she', as_float(weights), as_float(g_block))
        grad_v = grad_v + jnp.einsum('shd,hde->she', as_float(k_block), as_float(r_block))
        return (grad_q.astype(jnp.bfloat16), grad_k.astype(jnp.bfloat16), grad_v.astype(jnp.bfloat16))
    grad_q, grad_k, grad_v = lax.map(backward_block, (q_blocks, k_blocks, v_blocks, state_round, after_round, grad_mixture))
    shape_out = (TOKENS, width_all)
    return (attended.reshape(shape_out), grad_q.reshape(shape_out), grad_k.reshape(shape_out), grad_v.reshape(shape_out))
```

```python
import functools

import jax
import jax.numpy as jnp
from jax import lax
from jax.experimental import pallas as pl
from jax.experimental.pallas import tpu as pltpu
from jax.sharding import PartitionSpec as P

HEADS = 32
HEAD_DIM = 128
EPSILON = 1e-05
BF = jnp.bfloat16
F32 = jnp.float32

CORES = 2


def dot(a, b, ca, cb):
    return lax.dot_general(a, b, (((ca,), (cb,)), ((), ())), preferred_element_type=F32)


def call(kernel, outs, args, flops, vmem=24):
    whole = pl.BlockSpec(memory_space=pltpu.VMEM)
    nbytes = sum(a.size * a.dtype.itemsize for a in args)
    nbytes += sum(o.size * o.dtype.itemsize for o in outs)
    return pl.pallas_call(
        kernel,
        out_shape=outs,
        in_specs=[whole] * len(args),
        out_specs=[whole] * len(outs),
        compiler_params=pltpu.CompilerParams(vmem_limit_bytes=vmem << 20),
        cost_estimate=pl.CostEstimate(flops=flops, bytes_accessed=nbytes, transcendentals=0),
    )(*args)


def cols(h):
    return pl.ds(pl.multiple_of(h * HEAD_DIM, HEAD_DIM), HEAD_DIM)


def state_kernel(a_ref, b_ref, s_ref):
    heads = a_ref.shape[1] // HEAD_DIM

    def one(h, _):
        s_ref[cols(h), :] = dot(a_ref[:, cols(h)], b_ref[:, cols(h)], 0, 0)
        return 0

    lax.fori_loop(0, heads, one, 0)


def triangle(n):
    rows = lax.broadcasted_iota(jnp.int32, (n, n), 0)
    return lax.broadcasted_iota(jnp.int32, (n, n), 1) <= rows


def lower(a, b):
    n = a.shape[0] // 2
    keep = triangle(n)
    top = jnp.where(keep, dot(a[:n], b[:n], 1, 1), 0.0).astype(BF)
    left = dot(a[n:], b[:n], 1, 1).astype(BF)
    right = jnp.where(keep, dot(a[n:], b[n:], 1, 1), 0.0).astype(BF)
    return top, left, right


def times(w, v):
    n = v.shape[0] // 2
    top, left, right = w
    return dot(top, v[:n], 1, 0), dot(left, v[:n], 1, 0) + dot(right, v[n:], 1, 0)


def times_t(w, v):
    n = v.shape[0] // 2
    top, left, right = w
    return dot(top, v[:n], 0, 0) + dot(left, v[n:], 0, 0), dot(right, v[n:], 0, 0)


def intra_kernel(q_ref, k_ref, v_ref, o_ref):
    n = q_ref.shape[0] // 2

    def one(h, _):
        c = cols(h)
        w = lower(q_ref[:, c], k_ref[:, c])
        a, b = times(w, v_ref[:, c])
        o_ref[:n, c] = a
        o_ref[n:, c] = b
        return 0

    lax.fori_loop(0, q_ref.shape[1] // HEAD_DIM, one, 0)


def mix_kernel(q_ref, s_ref, i_ref, c_ref, g_ref, m_ref, p_ref, sq_ref, pr_ref):
    length = q_ref.shape[0]
    sq_ref[...] = jnp.zeros_like(sq_ref)
    pr_ref[...] = jnp.zeros_like(pr_ref)

    def one(h, _):
        c = cols(h)
        m = i_ref[:, c] + dot(q_ref[:, c], s_ref[c, :].astype(BF), 1, 0)
        m_ref[:, c] = m
        sq_ref[...] += m * m
        pr_ref[...] += (c_ref[:, c].astype(F32) * g_ref[:, c]) * m
        return 0

    lax.fori_loop(0, q_ref.shape[1] // HEAD_DIM, one, 0)
    for i in range(length // 128):
        rows = pl.ds(i * 128, 128)
        p_ref[pl.ds(i, 1), :] = jnp.sum(sq_ref[rows, :].T, axis=0, keepdims=True)
        p_ref[pl.ds(4 + i, 1), :] = jnp.sum(pr_ref[rows, :].T, axis=0, keepdims=True)


def spread(row):
    return jnp.broadcast_to(row, (128, 128)).T


def grad_kernel(q_ref, m_ref, c_ref, g_ref, p0, p1, p2, p3, gm_ref, b_ref, n_ref, inv_ref, cf_ref):
    width = HEADS * HEAD_DIM
    sums = p0[...] + p1[...] + p2[...] + p3[...]
    inverse = lax.rsqrt(sums[:4] / width + EPSILON)
    coef = inverse * inverse * inverse * sums[4:] / width
    for i in range(4):
        rows = pl.ds(i * 128, 128)
        inv_ref[rows, :] = spread(inverse[i : i + 1])
        cf_ref[rows, :] = spread(coef[i : i + 1])
    n_ref[...] = inv_ref[...]

    def one(h, _):
        c = cols(h)
        scaled = c_ref[:, c].astype(F32) * g_ref[:, c]
        gm = (inv_ref[...] * scaled - m_ref[:, c] * cf_ref[...]).astype(BF)
        gm_ref[:, c] = gm
        b_ref[c, :] = dot(q_ref[:, c], gm, 0, 0)
        return 0

    lax.fori_loop(0, q_ref.shape[1] // HEAD_DIM, one, 0)


def back_kernel(q_ref, k_ref, v_ref, gm_ref, s_ref, m_ref, n_ref, g_ref, at_ref, gq_ref, gk_ref, gv_ref):
    n = q_ref.shape[0] // 2

    def one(h, _):
        c = cols(h)
        at_ref[:, c] = (m_ref[:, c] * n_ref[...] * g_ref[:, c]).astype(BF)
        q, k, v, gm = q_ref[:, c], k_ref[:, c], v_ref[:, c], gm_ref[:, c]
        gw = lower(gm, v)
        a, b = times(gw, k)
        s = s_ref[c, :].astype(BF)
        gq_ref[:n, c] = (a + dot(gm[:n], s, 1, 1)).astype(BF)
        gq_ref[n:, c] = (b + dot(gm[n:], s, 1, 1)).astype(BF)
        a, b = times_t(gw, q)
        gk_ref[:n, c] = a
        gk_ref[n:, c] = b
        a, b = times_t(lower(q, k), gm)
        gv_ref[:n, c] = a
        gv_ref[n:, c] = b
        return 0

    lax.fori_loop(0, q_ref.shape[1] // HEAD_DIM, one, 0)


def last_kernel(k_ref, v_ref, a_ref, gki_ref, gvi_ref, gk_ref, gv_ref):
    def one(h, _):
        c = cols(h)
        a = a_ref[c, :].astype(BF)
        gk_ref[:, c] = (gki_ref[:, c] + dot(v_ref[:, c], a, 1, 1)).astype(BF)
        gv_ref[:, c] = (gvi_ref[:, c] + dot(k_ref[:, c], a, 1, 0)).astype(BF)
        return 0

    lax.fori_loop(0, k_ref.shape[1] // HEAD_DIM, one, 0)


def running_kernel(reverse, g_ref, o_ref):
    n = g_ref.shape[0]
    total = jnp.zeros(g_ref.shape[1:], F32)
    order = list(range(n))
    if reverse:
        order.reverse()
    for i in order:
        o_ref[i] = total
        if i != order[-1]:
            total = total + g_ref[i]


def carried(part, reverse):
    count = lax.axis_size("ctx")
    chips = count // CORES
    core = lax.rem(lax.axis_index("ctx"), CORES)
    swap = [(i, i ^ 1) for i in range(count)]
    groups = [[i * CORES + c for i in range(chips)] for c in range(CORES)]
    half = part.shape[0] // 2
    first, second = part[:half], part[half:]
    keep = jnp.where(core == 0, first, second)
    other = lax.ppermute(jnp.where(core == 0, second, first), "ctx", swap)
    ahead = jnp.where((core == 0) != reverse, keep, other)
    pieces = (keep + other).reshape(chips, -1, HEAD_DIM)
    pieces = lax.all_to_all(pieces, "ctx", 0, 0, axis_index_groups=groups)
    (pieces,) = call(
        functools.partial(running_kernel, reverse),
        [jax.ShapeDtypeStruct(pieces.shape, F32)],
        [pieces],
        pieces.size,
        4,
    )
    pieces = lax.all_to_all(pieces, "ctx", 0, 0, axis_index_groups=groups)
    near = pieces.reshape(half, HEAD_DIM)
    far = near + ahead
    mine = jnp.where((core == 0) != reverse, near, far)
    theirs = jnp.where((core == 0) != reverse, far, near)
    theirs = lax.ppermute(theirs, "ctx", swap)
    return jnp.concatenate(
        [jnp.where(core == 0, mine, theirs), jnp.where(core == 0, theirs, mine)], axis=0
    )


def body(query, keys, values, gain, cotangent):
    length, width = query.shape
    square = 2 * length * length * width
    small = 2 * length * HEAD_DIM * width
    gain = gain.reshape(1, width)
    shape = lambda dtype: jax.ShapeDtypeStruct((length, width), dtype)
    states = jax.ShapeDtypeStruct((width, HEAD_DIM), F32)
    rows = jax.ShapeDtypeStruct((8, 128), F32)

    (local,) = call(state_kernel, [states], [keys, values], small)
    before = carried(local, False)
    (intra,) = call(intra_kernel, [shape(F32)], [query, keys, values], 2 * square)
    lanes = pltpu.VMEM((length, 128), F32)
    whole = pl.BlockSpec(memory_space=pltpu.VMEM)
    mixture, sums = pl.pallas_call(
        mix_kernel,
        out_shape=[shape(F32), rows],
        in_specs=[whole] * 5,
        out_specs=[whole] * 2,
        scratch_shapes=[lanes, lanes],
        compiler_params=pltpu.CompilerParams(vmem_limit_bytes=24 << 20),
    )(query, before, intra, cotangent, gain)
    heads = lax.axis_size("head")
    others = [
        lax.ppermute(sums, "head", [(i, i ^ j) for i in range(heads)]) for j in (1, 3, 2)
    ]
    grad_mixture, back, inverse = pl.pallas_call(
        grad_kernel,
        out_shape=[shape(BF), states, jax.ShapeDtypeStruct((length, 128), F32)],
        in_specs=[whole] * 8,
        out_specs=[whole] * 3,
        scratch_shapes=[lanes, lanes],
        compiler_params=pltpu.CompilerParams(vmem_limit_bytes=24 << 20),
    )(query, mixture, cotangent, gain, sums, *others)
    after = carried(back, True)
    attended, grad_q, grad_k, grad_v = call(
        back_kernel,
        [shape(BF), shape(BF), shape(F32), shape(F32)],
        [query, keys, values, grad_mixture, before, mixture, inverse, gain],
        5 * square,
    )
    grad_k, grad_v = call(
        last_kernel, [shape(BF), shape(BF)], [keys, values, after, grad_k, grad_v], 2 * small
    )
    return attended, grad_q, grad_k, grad_v


def solution(mesh):
    spec = P("ctx", "head")
    return jax.shard_map(
        body,
        mesh=mesh,
        in_specs=(spec, spec, spec, P("head"), spec),
        out_specs=(spec,) * 4,
        check_vma=False,
    )
```

```python
import functools

import jax
import jax.numpy as jnp
from jax import lax
from jax.experimental import pallas as pl
from jax.experimental.pallas import tpu as pltpu
from jax.sharding import PartitionSpec as P

HEADS = 32
HEAD_DIM = 128
EPSILON = 1e-05
BF = jnp.bfloat16
F32 = jnp.float32

X = 4
CORES = 2
PAIR = 2 * X

VMEM = pl.BlockSpec(memory_space=pltpu.VMEM)
HBM = pl.BlockSpec(memory_space=pltpu.HBM)
ANY = pl.BlockSpec(memory_space=pl.ANY)


def dot(a, b, ca, cb):
    return lax.dot_general(a, b, (((ca,), (cb,)), ((), ())), preferred_element_type=F32)


def call(kernel, outs, args, flops, after=(), ins=VMEM, out=VMEM, scratch=(), vmem=16):
    nbytes = sum(a.size * a.dtype.itemsize for a in args)
    nbytes += sum(o.size * o.dtype.itemsize for o in outs)

    def body(*refs):
        kernel(*refs[: len(args)], *refs[len(args) + len(after) :])

    return pl.pallas_call(
        body,
        out_shape=outs,
        in_specs=[ins] * len(args) + [ANY] * len(after),
        out_specs=[out] * len(outs),
        scratch_shapes=list(scratch),
        compiler_params=pltpu.CompilerParams(vmem_limit_bytes=vmem << 20),
        cost_estimate=pl.CostEstimate(flops=flops, bytes_accessed=nbytes, transcendentals=0),
    )(*args, *after)


def array(shape, dtype):
    return jax.ShapeDtypeStruct(shape, dtype)


def at(h):
    return slice(h * HEAD_DIM, (h + 1) * HEAD_DIM)


def my_core():
    return lax.rem(lax.axis_index("ctx"), CORES)


def put(h, half, value, keep_ref, send_ref):
    mine = my_core() == h // half
    rows = at(h % half)

    @pl.when(mine)
    def _():
        keep_ref[rows, :] = value

    @pl.when(jnp.logical_not(mine))
    def _():
        send_ref[rows, :] = value


def join(mine_ref, theirs_ref, out_ref):
    half = mine_ref.shape[0]
    first = my_core() == 0
    mine, theirs = mine_ref[...].astype(BF), theirs_ref[...].astype(BF)
    out_ref[:half] = jnp.where(first, mine, theirs)
    out_ref[half:] = jnp.where(first, theirs, mine)


CHUNK = 2


def state_kernel(a_hbm, b_hbm, keep_ref, send_ref, a_ref, b_ref, sems):
    heads = a_ref.shape[1] // HEAD_DIM
    copies = []
    for i in range(0, heads, CHUNK):
        c = slice(i * HEAD_DIM, (i + CHUNK) * HEAD_DIM)
        for j, (src, dst) in enumerate(((a_hbm, a_ref), (b_hbm, b_ref))):
            copy = pltpu.make_async_copy(src.at[:, c], dst.at[:, c], sems.at[i // CHUNK, j])
            copy.start()
            copies.append(copy)
    for h in range(heads):
        if h % CHUNK == 0:
            copies[h // CHUNK * 2].wait()
            copies[h // CHUNK * 2 + 1].wait()
        put(h, heads // 2, dot(a_ref[:, at(h)], b_ref[:, at(h)], 0, 0), keep_ref, send_ref)


def triangle(n, flip=False):
    rows = lax.broadcasted_iota(jnp.int32, (n, n), 0)
    cols = lax.broadcasted_iota(jnp.int32, (n, n), 1)
    return rows <= cols if flip else cols <= rows


def lower(a, b):
    n = a.shape[0] // 2
    keep = triangle(n)
    top = jnp.where(keep, dot(a[:n], b[:n], 1, 1), 0.0).astype(BF)
    left = dot(a[n:], b[:n], 1, 1).astype(BF)
    right = jnp.where(keep, dot(a[n:], b[n:], 1, 1), 0.0).astype(BF)
    return top, left, right


def lower_t(a, b):
    n = a.shape[0] // 2
    keep = triangle(n, True)
    top = jnp.where(keep, dot(b[:n], a[:n], 1, 1), 0.0).astype(BF)
    left = dot(b[:n], a[n:], 1, 1).astype(BF)
    right = jnp.where(keep, dot(b[n:], a[n:], 1, 1), 0.0).astype(BF)
    return top, left, right


def intra_kernel(heads, q_ref, k_ref, v_ref, qt_ref, wt_ref, o_ref):
    n = q_ref.shape[0] // 2
    for i, h in enumerate(heads):
        q, k, v = q_ref[:, at(h)], k_ref[:, at(h)], v_ref[:, at(h)]
        qt_ref[at(i), :] = q.T
        top, left, right = lower(q, k)
        o_ref[:n, at(i)] = dot(top, v[:n], 1, 0)
        o_ref[n:, at(i)] = dot(left, v[:n], 1, 0) + dot(right, v[n:], 1, 0)
        for j, block in enumerate(lower_t(q, k)):
            wt_ref[3 * i + j] = block


def mix_kernel(parts, *refs):
    q_ref, mine_ref, theirs_ref, c_ref, g_ref = refs[:5]
    i_refs = refs[5 : 5 + len(parts)]
    m_ref, r_ref, p_ref = refs[5 + len(parts) :]
    join(mine_ref, theirs_ref, r_ref)
    for i in range(q_ref.shape[0] // 128):
        rows = slice(i * 128, (i + 1) * 128)
        squares = jnp.zeros((128, HEAD_DIM), F32)
        products = jnp.zeros((128, HEAD_DIM), F32)
        for heads, i_ref in zip(parts, i_refs):
            for j, h in enumerate(heads):
                m = i_ref[rows, at(j)] + dot(q_ref[rows, at(h)], r_ref[at(h), :], 1, 0)
                m_ref[rows, at(h)] = m
                squares = squares + m * m
                products = products + (c_ref[rows, at(h)].astype(F32) * g_ref[:, at(h)]) * m
        p_ref[i : i + 1, :] = jnp.sum(squares.T, axis=0, keepdims=True)
        p_ref[4 + i : 5 + i, :] = jnp.sum(products.T, axis=0, keepdims=True)


def spread(row):
    return jnp.broadcast_to(row, (128, 128)).T


def grad_kernel(parts, *refs):
    m_ref, c_ref, g_ref, p0, p1, p2, p3 = refs[:7]
    t_refs = refs[7 : 7 + len(parts)]
    gm_ref, n_ref, keep_ref, send_ref = refs[7 + len(parts) :]
    width = HEADS * HEAD_DIM
    sums = p0[...] + p1[...] + p2[...] + p3[...]
    inverse = lax.rsqrt(sums[:4] / width + EPSILON)
    coef = inverse * inverse * inverse * sums[4:] / width
    count = m_ref.shape[1] // HEAD_DIM
    for i in range(4):
        rows = slice(i * 128, (i + 1) * 128)
        inv = spread(inverse[i : i + 1])
        cf = spread(coef[i : i + 1])
        n_ref[rows, :] = inv
        for h in range(count):
            scaled = c_ref[rows, at(h)].astype(F32) * g_ref[:, at(h)]
            gm_ref[rows, at(h)] = (inv * scaled - m_ref[rows, at(h)] * cf).astype(BF)
    for heads, t_ref in zip(parts, t_refs):
        for j, h in enumerate(heads):
            put(h, count // 2, dot(t_ref[at(j), :], gm_ref[:, at(h)], 1, 0), keep_ref, send_ref)


def back_kernel(heads, parts, *refs):
    q_ref, k_ref, v_ref, gm_ref, r_ref, m_ref, n_ref, g_ref = refs[:8]
    w_refs = refs[8 : 8 + len(parts)]
    at_ref, gq_ref, gk_ref, gv_ref = refs[8 + len(parts) :]
    n = q_ref.shape[0] // 2
    for i, h in enumerate(heads):
        at_ref[:, at(i)] = (m_ref[:, at(h)] * n_ref[...] * g_ref[:, at(h)]).astype(BF)
        q, k, v, gm = q_ref[:, at(h)], k_ref[:, at(h)], v_ref[:, at(h)], gm_ref[:, at(h)]
        top, left, right = lower(gm, v)
        s = r_ref[at(h), :]
        gq_ref[:n, at(i)] = (dot(top, k[:n], 1, 0) + dot(gm[:n], s, 1, 1)).astype(BF)
        gq_ref[n:, at(i)] = (
            dot(left, k[:n], 1, 0) + dot(right, k[n:], 1, 0) + dot(gm[n:], s, 1, 1)
        ).astype(BF)
        gk_ref[:n, at(i)] = dot(top, q[:n], 0, 0) + dot(left, q[n:], 0, 0)
        gk_ref[n:, at(i)] = dot(right, q[n:], 0, 0)
        (w_ref, j) = next((r, p.index(h)) for r, p in zip(w_refs, parts) if h in p)
        top, left, right = w_ref[3 * j], w_ref[3 * j + 1], w_ref[3 * j + 2]
        gv_ref[:n, at(i)] = dot(top, gm[:n], 1, 0) + dot(left, gm[n:], 1, 0)
        gv_ref[n:, at(i)] = dot(right, gm[n:], 1, 0)


def flush_kernel(parts, *refs):
    k = len(parts)
    pieces, outs, sems = refs[: 2 * k], refs[2 * k : 2 * k + 2], refs[-1]
    copies = []
    for i, heads in enumerate(parts):
        c = slice(heads[0] * HEAD_DIM, (heads[-1] + 1) * HEAD_DIM)
        for j in range(2):
            copy = pltpu.make_async_copy(pieces[j * k + i], outs[j].at[:, c], sems.at[i, j])
            copy.start()
            copies.append(copy)
    for copy in copies:
        copy.wait()


def last_kernel(parts, *refs):
    k_ref, v_ref, mine_ref, theirs_ref = refs[:4]
    n = len(parts)
    gki, gvi = refs[4 : 4 + n], refs[4 + n : 4 + 2 * n]
    gk_hbm, gv_hbm, gk_ref, gv_ref, r_ref, sems = refs[4 + 2 * n :]
    join(mine_ref, theirs_ref, r_ref)
    copies = []
    for heads, gki_ref, gvi_ref in zip(parts, gki, gvi):
        for j, h in enumerate(heads):
            a = r_ref[at(h), :]
            gk_ref[:, at(h)] = (gki_ref[:, at(j)] + dot(v_ref[:, at(h)], a, 1, 1)).astype(BF)
            gv_ref[:, at(h)] = (gvi_ref[:, at(j)] + dot(k_ref[:, at(h)], a, 1, 0)).astype(BF)
            if h % CHUNK == CHUNK - 1:
                c = slice((h - CHUNK + 1) * HEAD_DIM, (h + 1) * HEAD_DIM)
                for i, (src, dst) in enumerate(((gk_ref, gk_hbm), (gv_ref, gv_hbm))):
                    copy = pltpu.make_async_copy(
                        src.at[:, c], dst.at[:, c], sems.at[h // CHUNK, i]
                    )
                    copy.start()
                    copies.append(copy)
    for copy in copies:
        copy.wait()


def add_kernel(a_ref, b_ref, o_ref):
    o_ref[...] = (a_ref[...] + b_ref[...]).reshape(o_ref.shape)


def finish_kernel(reverse, g_ref, keep_ref, other_ref, mine_ref, give_ref):
    first = g_ref[...].reshape(keep_ref.shape)
    leads = my_core() == (1 if reverse else 0)
    second = first + jnp.where(leads, keep_ref[...], other_ref[...])
    mine_ref[...] = jnp.where(leads, first, second)
    give_ref[...] = jnp.where(leads, second, first)


def running_kernel(reverse, g_ref, o_ref, t_ref):
    total = jnp.zeros(g_ref.shape[1:], F32)
    for i in range(g_ref.shape[0]) if not reverse else reversed(range(g_ref.shape[0])):
        o_ref[i] = total
        total = total + g_ref[i]
    t_ref[...] = total


def outer_kernel(reverse, g_ref, near_ref, far_ref, o_ref):
    z = lax.axis_index("ctx") // (X * CORES)
    bit = 0 if reverse else 1
    near, far = lax.rem(z // 2, 2) == bit, z // 4 == bit
    total = jnp.where(near, near_ref[...], 0.0) + jnp.where(far, far_ref[...], 0.0)
    for i in range(g_ref.shape[0]):
        o_ref[i] = g_ref[i] + total


def carried(keep, send, reverse, windows):
    count = lax.axis_size("ctx")
    plane = X * CORES
    pieces_of = (PAIR, keep.shape[0] // PAIR, HEAD_DIM)
    swap = [(i, i ^ 1) for i in range(count)]
    groups = [
        [pair * PAIR * CORES + i * CORES + c for i in range(PAIR)]
        for pair in range(count // (PAIR * CORES))
        for c in range(CORES)
    ]
    near_z = [(i, (i // plane ^ 2) * plane + i % plane) for i in range(count)]
    across = (6, 7, 4, 5, 2, 3, 0, 1)
    far_z = [(i, across[i // plane] * plane + i % plane) for i in range(count)]
    made = []

    def window(i, operand):
        made.append(windows[i](operand))
        return made[-1][-1:]

    def add(a, b, after, shape):
        return call(add_kernel, [array(shape, F32)], [a, b], a.size, after, vmem=4)[0]

    other = lax.ppermute(send, "ctx", swap)
    after = window(0, send)
    pieces = add(keep, other, after, pieces_of)
    pieces = lax.all_to_all(pieces, "ctx", 0, 0, axis_index_groups=groups)
    inner, total = call(
        functools.partial(running_kernel, reverse),
        [array(pieces.shape, F32), array(pieces.shape[1:], F32)],
        [pieces],
        pieces.size,
        vmem=4,
    )
    near = lax.ppermute(total, "ctx", near_z)
    after = window(1, total)
    total = add(total, near, after, total.shape)
    far = lax.ppermute(total, "ctx", far_z)
    after = window(2, total)
    (pieces,) = call(
        functools.partial(outer_kernel, reverse),
        [array(pieces.shape, F32)],
        [inner, near, far],
        pieces.size,
        after,
        vmem=4,
    )
    pieces = lax.all_to_all(pieces, "ctx", 0, 0, axis_index_groups=groups)
    mine, give = call(
        functools.partial(finish_kernel, reverse),
        [array(keep.shape, F32)] * 2,
        [pieces, keep, other],
        pieces.size,
        vmem=4,
    )
    theirs = lax.ppermute(give, "ctx", swap)
    window(3, give)
    return mine, theirs, made


def body(query, keys, values, gain, cotangent):
    length, width = query.shape
    count = width // HEAD_DIM
    square = 2 * length * length * HEAD_DIM
    small = 2 * length * HEAD_DIM * width
    gain = gain.reshape(1, width)
    whole = lambda dtype: array((length, width), dtype)
    part = lambda heads, dtype: array((length, len(heads) * HEAD_DIM), dtype)
    half = array((width // 2, HEAD_DIM), F32)
    rounded = array((width, HEAD_DIM), BF)
    copied = [pltpu.VMEM((length, width), BF)] * 2
    sems = pltpu.SemaphoreType.DMA((count // CHUNK, 2))
    nothing = lambda ready: [ready]

    keep, send = call(
        state_kernel,
        [half, half],
        [pltpu.with_memory_space_constraint(a, pltpu.HBM) for a in (keys, values)],
        small,
        ins=HBM,
        scratch=copied + [sems],
        vmem=24,
    )

    ahead = [list(range(count // 2)), list(range(count // 2, count))]

    def intra_piece(heads):
        return lambda ready: call(
            functools.partial(intra_kernel, heads),
            [
                array((len(heads) * HEAD_DIM, length), BF),
                array((3 * len(heads), length // 2, length // 2), BF),
                part(heads, F32),
            ],
            [query, keys, values],
            3 * square * len(heads),
            [ready],
        )

    mine, theirs, made = carried(
        keep, send, False, [nothing, intra_piece(ahead[0]), intra_piece(ahead[1]), nothing]
    )
    query_t, weights_t, mixed = zip(*made[1:3])
    mixture, state, sums = call(
        functools.partial(mix_kernel, ahead),
        [whole(F32), rounded, array((8, 128), F32)],
        [query, mine, theirs, cotangent, gain, *mixed],
        small,
    )
    heads = lax.axis_size("head")
    others = [
        lax.ppermute(sums, "head", [(i, i ^ j) for i in range(heads)]) for j in (1, 3, 2)
    ]
    grad_mixture, inverse, keep, send = call(
        functools.partial(grad_kernel, ahead),
        [whole(BF), array((length, 128), F32), half, half],
        [mixture, cotangent, gain, sums, *others, *query_t],
        small,
    )
    behind = [list(range(2)), list(range(2, 5)), list(range(5, count))]

    def back_piece(heads):
        return lambda ready: call(
            functools.partial(back_kernel, heads, ahead),
            [part(heads, BF), part(heads, BF), part(heads, F32), part(heads, F32)],
            [query, keys, values, grad_mixture, state, mixture, inverse, gain, *weights_t],
            4 * square * len(heads),
            [ready],
        )

    flushed = []
    pieces = []

    def kept(heads):
        def one(ready):
            pieces.append(back_piece(heads)(ready))
            return pieces[-1]

        return one

    def flush(ready):
        attended, grad_q = zip(*[p[:2] for p in pieces])
        flushed.extend(
            call(
                functools.partial(flush_kernel, behind),
                [whole(BF), whole(BF)],
                [*attended, *grad_q],
                small,
                [ready],
                out=HBM,
                scratch=[pltpu.SemaphoreType.DMA((len(behind), 2))],
            )
        )
        return flushed

    mine, theirs, _ = carried(keep, send, True, [*map(kept, behind), flush])
    attended, grad_q = flushed
    grad_k, grad_v = call(
        functools.partial(last_kernel, behind),
        [whole(BF), whole(BF)],
        [keys, values, mine, theirs, *[p[2] for p in pieces], *[p[3] for p in pieces]],
        2 * small,
        [attended],
        out=HBM,
        scratch=copied + [pltpu.VMEM((width, HEAD_DIM), BF), sems],
    )
    return attended, grad_q, grad_k, grad_v


def solution(mesh):
    spec = P("ctx", "head")
    return jax.shard_map(
        body,
        mesh=mesh,
        in_specs=(spec, spec, spec, P("head"), spec),
        out_specs=(spec,) * 4,
        check_vma=False,
    )
```

```python
import functools

import jax
import jax.numpy as jnp
from jax import lax
from jax.experimental import pallas as pl
from jax.experimental.pallas import tpu as pltpu
from jax.sharding import PartitionSpec as P

HEADS = 32
HEAD_DIM = 128
EPSILON = 1e-05
BF = jnp.bfloat16
F32 = jnp.float32

X = 4
CORES = 2
PAIR = 2 * X

VMEM = pl.BlockSpec(memory_space=pltpu.VMEM)
HBM = pl.BlockSpec(memory_space=pltpu.HBM)
ANY = pl.BlockSpec(memory_space=pl.ANY)


def dot(a, b, ca, cb):
    return lax.dot_general(a, b, (((ca,), (cb,)), ((), ())), preferred_element_type=F32)


def call(kernel, outs, args, flops, after=(), ins=VMEM, out=VMEM, scratch=(), vmem=16):
    nbytes = sum(a.size * a.dtype.itemsize for a in args)
    nbytes += sum(o.size * o.dtype.itemsize for o in outs)

    def body(*refs):
        kernel(*refs[: len(args)], *refs[len(args) + len(after) :])

    return pl.pallas_call(
        body,
        out_shape=outs,
        in_specs=[ins] * len(args) + [ANY] * len(after),
        out_specs=[out] * len(outs),
        scratch_shapes=list(scratch),
        compiler_params=pltpu.CompilerParams(vmem_limit_bytes=vmem << 20),
        cost_estimate=pl.CostEstimate(flops=flops, bytes_accessed=nbytes, transcendentals=0),
    )(*args, *after)


def array(shape, dtype):
    return jax.ShapeDtypeStruct(shape, dtype)


def at(h):
    return slice(h * HEAD_DIM, (h + 1) * HEAD_DIM)


def my_core():
    return lax.rem(lax.axis_index("ctx"), CORES)


def shift(i):
    return i // (2 * X * CORES)


def my_half():
    i = lax.axis_index("ctx")
    return lax.rem(i % CORES + shift(i), 2)


OWN, OTHER = 0, 1


def cols(side, j, half):
    mine = my_half()
    base = (mine if side == OWN else 1 - mine) * (half * HEAD_DIM)
    return pl.ds(pl.multiple_of(base + j * HEAD_DIM, HEAD_DIM), HEAD_DIM)


def state_own_kernel(side, a_ref, b_ref, s_ref):
    half = s_ref.shape[0] // HEAD_DIM
    for j in range(half):
        c = cols(side, j, half)
        s_ref[at(j), :] = dot(a_ref[:, c], b_ref[:, c], 0, 0)


def state_kernel(side, a_hbm, b_hbm, s_ref, a_ref, b_ref, sems):
    half = a_ref.shape[1] // HEAD_DIM
    copies = []
    for j in range(half):
        for i, (src, dst) in enumerate(((a_hbm, a_ref), (b_hbm, b_ref))):
            copy = pltpu.make_async_copy(
                src.at[:, cols(side, j, half)], dst.at[:, at(j)], sems.at[i, j]
            )
            copy.start()
            copies.append(copy)
    for j in range(half):
        copies[2 * j].wait()
        copies[2 * j + 1].wait()
        s_ref[at(j), :] = dot(a_ref[:, at(j)], b_ref[:, at(j)], 0, 0)


def triangle(n, flip=False):
    rows = lax.broadcasted_iota(jnp.int32, (n, n), 0)
    cols = lax.broadcasted_iota(jnp.int32, (n, n), 1)
    return rows <= cols if flip else cols <= rows


def lower(a, b):
    n = a.shape[0] // 2
    keep = triangle(n)
    top = jnp.where(keep, dot(a[:n], b[:n], 1, 1), 0.0).astype(BF)
    left = dot(a[n:], b[:n], 1, 1).astype(BF)
    right = jnp.where(keep, dot(a[n:], b[n:], 1, 1), 0.0).astype(BF)
    return top, left, right


def lower_t(a, b):
    n = a.shape[0] // 2
    keep = triangle(n, True)
    top = jnp.where(keep, dot(b[:n], a[:n], 1, 1), 0.0).astype(BF)
    left = dot(b[:n], a[n:], 1, 1).astype(BF)
    right = jnp.where(keep, dot(b[n:], a[n:], 1, 1), 0.0).astype(BF)
    return top, left, right


def intra_kernel(side, q_ref, k_ref, v_ref, qt_ref, wt_ref, o_ref):
    n = q_ref.shape[0] // 2
    half = o_ref.shape[1] // HEAD_DIM
    for j in range(half):
        c = cols(side, j, half)
        q, k, v = q_ref[:, c], k_ref[:, c], v_ref[:, c]
        qt_ref[at(j), :] = q.T
        top, left, right = lower(q, k)
        o_ref[:n, at(j)] = dot(top, v[:n], 1, 0)
        o_ref[n:, at(j)] = dot(left, v[:n], 1, 0) + dot(right, v[n:], 1, 0)
        for i, block in enumerate(lower_t(q, k)):
            wt_ref[3 * j + i] = block


def mix_kernel(side, q_ref, s_ref, i_ref, c_ref, g_ref, *refs):
    before_ref = refs[0] if side == OTHER else None
    m_ref, p_ref = refs[-2:]
    half = m_ref.shape[1] // HEAD_DIM
    state = [s_ref[at(j), :].astype(BF) for j in range(half)]
    for i in range(q_ref.shape[0] // 128):
        rows = slice(i * 128, (i + 1) * 128)
        squares = jnp.zeros((128, HEAD_DIM), F32)
        products = jnp.zeros((128, HEAD_DIM), F32)
        for j in range(half):
            c = cols(side, j, half)
            m = i_ref[rows, at(j)] + dot(q_ref[rows, c], state[j], 1, 0)
            m_ref[rows, at(j)] = m
            squares = squares + m * m
            products = products + (c_ref[rows, c].astype(F32) * g_ref[:, c]) * m
        for row, value in ((i, squares), (4 + i, products)):
            value = jnp.sum(value.T, axis=0, keepdims=True)
            if side == OTHER:
                value = value + before_ref[row : row + 1, :]
            p_ref[row : row + 1, :] = value


def spread(row):
    return jnp.broadcast_to(row, (128, 128)).T


def grad(side, qt_ref, m_ref, c_ref, g_ref, inv_ref, cf_ref, gm_ref, s_ref):
    half = m_ref.shape[1] // HEAD_DIM
    for j in range(half):
        c = cols(side, j, half)
        scaled = c_ref[:, c].astype(F32) * g_ref[:, c]
        gm = (inv_ref[...] * scaled - m_ref[:, at(j)] * cf_ref[...]).astype(BF)
        gm_ref[:, at(j)] = gm
        s_ref[at(j), :] = dot(qt_ref[at(j), :], gm, 1, 0)


def grad_other_kernel(qt_ref, m_ref, c_ref, g_ref, p0, p1, p2, p3, gm_ref, s_ref, inv_ref, cf_ref):
    width = HEADS * HEAD_DIM
    sums = p0[...] + p1[...] + p2[...] + p3[...]
    inverse = lax.rsqrt(sums[:4] / width + EPSILON)
    coef = inverse * inverse * inverse * sums[4:] / width
    for i in range(4):
        rows = slice(i * 128, (i + 1) * 128)
        inv_ref[rows, :] = spread(inverse[i : i + 1])
        cf_ref[rows, :] = spread(coef[i : i + 1])
    grad(OTHER, qt_ref, m_ref, c_ref, g_ref, inv_ref, cf_ref, gm_ref, s_ref)


def grad_own_kernel(qt_ref, m_ref, c_ref, g_ref, inv_ref, cf_ref, gm_ref, s_ref):
    grad(OWN, qt_ref, m_ref, c_ref, g_ref, inv_ref, cf_ref, gm_ref, s_ref)


def back_kernel(
    side, q_ref, k_ref, v_ref, gm_ref, s_ref, m_ref, inv_ref, g_ref, wt_ref,
    at_ref, gq_ref, gk_ref, gv_ref,
):
    n = q_ref.shape[0] // 2
    half = gm_ref.shape[1] // HEAD_DIM
    for j in range(half):
        c = cols(side, j, half)
        at_ref[:, at(j)] = (m_ref[:, at(j)] * inv_ref[...] * g_ref[:, c]).astype(BF)
        q, k, v, gm = q_ref[:, c], k_ref[:, c], v_ref[:, c], gm_ref[:, at(j)]
        top, left, right = lower(gm, v)
        s = s_ref[at(j), :].astype(BF)
        gq_ref[:n, at(j)] = (dot(top, k[:n], 1, 0) + dot(gm[:n], s, 1, 1)).astype(BF)
        gq_ref[n:, at(j)] = (
            dot(left, k[:n], 1, 0) + dot(right, k[n:], 1, 0) + dot(gm[n:], s, 1, 1)
        ).astype(BF)
        gk_ref[:n, at(j)] = dot(top, q[:n], 0, 0) + dot(left, q[n:], 0, 0)
        gk_ref[n:, at(j)] = dot(right, q[n:], 0, 0)
        top, left, right = wt_ref[3 * j], wt_ref[3 * j + 1], wt_ref[3 * j + 2]
        gv_ref[:n, at(j)] = dot(top, gm[:n], 1, 0) + dot(left, gm[n:], 1, 0)
        gv_ref[n:, at(j)] = dot(right, gm[n:], 1, 0)


def send_out(pairs, half, sems):
    mine = my_half()
    copies = []
    for i, (side, src, dst) in enumerate(pairs):
        base = (mine if side == OWN else 1 - mine) * (half * HEAD_DIM)
        c = pl.ds(pl.multiple_of(base, half * HEAD_DIM), half * HEAD_DIM)
        copies.append(pltpu.make_async_copy(src, dst.at[:, c], sems.at[i]))
        copies[-1].start()
    return copies


def last(side, k_ref, v_ref, s_ref, gki_ref, gvi_ref, gk_ref, gv_ref, then=lambda j: None):
    half = gki_ref.shape[1] // HEAD_DIM
    for j in range(half):
        c = cols(side, j, half)
        s = s_ref[at(j), :].astype(BF)
        gk_ref[:, at(j)] = (gki_ref[:, at(j)] + dot(v_ref[:, c], s, 1, 1)).astype(BF)
        gv_ref[:, at(j)] = (gvi_ref[:, at(j)] + dot(k_ref[:, c], s, 1, 0)).astype(BF)
        then(j)


def last_own_kernel(
    k_ref, v_ref, s_ref, gki_ref, gvi_ref, ato_ref, ats_ref, gqo_ref, gqs_ref,
    gk_ref, gv_ref, at_hbm, gq_hbm, sems,
):
    half = gki_ref.shape[1] // HEAD_DIM
    pairs = [
        (OWN, ato_ref, at_hbm), (OTHER, ats_ref, at_hbm),
        (OWN, gqo_ref, gq_hbm), (OTHER, gqs_ref, gq_hbm),
    ]
    copies = send_out(pairs, half, sems)
    last(OWN, k_ref, v_ref, s_ref, gki_ref, gvi_ref, gk_ref, gv_ref)
    for copy in copies:
        copy.wait()


def last_other_kernel(
    k_ref, v_ref, s_ref, gki_ref, gvi_ref, gko_ref, gvo_ref,
    gk_hbm, gv_hbm, gk_ref, gv_ref, sems, head_sems,
):
    half = gki_ref.shape[1] // HEAD_DIM
    copies = send_out([(OWN, gko_ref, gk_hbm), (OWN, gvo_ref, gv_hbm)], half, sems)

    def then(j):
        for i, (src, dst) in enumerate(((gk_ref, gk_hbm), (gv_ref, gv_hbm))):
            copy = pltpu.make_async_copy(
                src.at[:, at(j)], dst.at[:, cols(OTHER, j, half)], head_sems.at[i, j]
            )
            copy.start()
            copies.append(copy)

    last(OTHER, k_ref, v_ref, s_ref, gki_ref, gvi_ref, gk_ref, gv_ref, then)
    for copy in copies:
        copy.wait()


def add_kernel(a_ref, b_ref, o_ref):
    o_ref[...] = (a_ref[...] + b_ref[...]).reshape(o_ref.shape)


def finish_kernel(reverse, g_ref, keep_ref, other_ref, mine_ref, give_ref):
    first = g_ref[...].reshape(keep_ref.shape)
    leads = my_core() == (1 if reverse else 0)
    second = first + jnp.where(leads, keep_ref[...], other_ref[...])
    mine_ref[...] = jnp.where(leads, first, second)
    give_ref[...] = jnp.where(leads, second, first)


def running_kernel(reverse, g_ref, o_ref, t_ref):
    total = jnp.zeros(g_ref.shape[1:], F32)
    for i in range(g_ref.shape[0]) if not reverse else reversed(range(g_ref.shape[0])):
        o_ref[i] = total
        total = total + g_ref[i]
    t_ref[...] = total


def outer_kernel(reverse, g_ref, near_ref, far_ref, o_ref):
    z = lax.axis_index("ctx") // (X * CORES)
    bit = 0 if reverse else 1
    near, far = lax.rem(z // 2, 2) == bit, z // 4 == bit
    total = jnp.where(near, near_ref[...], 0.0) + jnp.where(far, far_ref[...], 0.0)
    for i in range(g_ref.shape[0]):
        o_ref[i] = g_ref[i] + total


def carried(send, reverse, windows):
    count = lax.axis_size("ctx")
    pieces_of = (PAIR, send.shape[0] // PAIR, HEAD_DIM)
    swap = [(i, i ^ 1) for i in range(count)]
    def on(chip, half):
        return chip * CORES + (half + shift(chip * CORES)) % CORES

    groups = [
        [on(pair * PAIR + i, half) for i in range(PAIR)]
        for pair in range(count // (PAIR * CORES))
        for half in range(2)
    ]
    across = (6, 7, 4, 5, 2, 3, 0, 1)

    def partners(of):
        chips = [(z * X + x, of(z) * X + x) for z in range(len(across)) for x in range(X)]
        return [(on(a, half), on(b, half)) for a, b in chips for half in range(2)]

    near_z = partners(lambda z: z ^ 2)
    far_z = partners(lambda z: across[z])

    def add(a, b, after, shape):
        return call(add_kernel, [array(shape, F32)], [a, b], a.size, after, vmem=4)[0]

    other = lax.ppermute(send, "ctx", swap)
    keep = windows[0](send)[-1]
    pieces = add(keep, other, (), pieces_of)
    pieces = lax.all_to_all(pieces, "ctx", 0, 0, axis_index_groups=groups)
    inner, total = call(
        functools.partial(running_kernel, reverse),
        [array(pieces.shape, F32), array(pieces.shape[1:], F32)],
        [pieces],
        pieces.size,
        vmem=4,
    )
    near = lax.ppermute(total, "ctx", near_z)
    after = windows[1](total)[-1:]
    total = add(total, near, after, total.shape)
    far = lax.ppermute(total, "ctx", far_z)
    after = windows[2](total)[-1:]
    (pieces,) = call(
        functools.partial(outer_kernel, reverse),
        [array(pieces.shape, F32)],
        [inner, near, far],
        pieces.size,
        after,
        vmem=4,
    )
    pieces = lax.all_to_all(pieces, "ctx", 0, 0, axis_index_groups=groups)
    mine, give = call(
        functools.partial(finish_kernel, reverse),
        [array(send.shape, F32)] * 2,
        [pieces, keep, other],
        pieces.size,
        vmem=4,
    )
    theirs = lax.ppermute(give, "ctx", swap)
    windows[3](give, mine)
    return mine, theirs


def body(query, keys, values, gain, cotangent):
    length, width = query.shape
    half = width // HEAD_DIM // 2
    square = 2 * length * length * HEAD_DIM * half
    small = 2 * length * HEAD_DIM * HEAD_DIM * half
    gain = gain.reshape(1, width)
    whole = array((length, width), BF)
    part = lambda dtype: array((length, half * HEAD_DIM), dtype)
    states = array((half * HEAD_DIM, HEAD_DIM), F32)
    lanes = array((length, HEAD_DIM), F32)
    rows = array((8, 128), F32)
    dmas = pltpu.SemaphoreType.DMA
    halves = [pltpu.VMEM((length, half * HEAD_DIM), BF)] * 2
    made = {}

    def made_by(name, side, kernel, outs, args, flops, after=(), **options):
        made[name, side] = call(functools.partial(kernel, side), outs, args, flops, after, **options)
        return made[name, side]

    in_hbm = [pltpu.with_memory_space_constraint(a, pltpu.HBM) for a in (keys, values)]

    (send,) = made_by(
        "state", OTHER, state_kernel, [states], in_hbm, small,
        ins=HBM, scratch=halves + [dmas((2, half))],
    )

    def state_own(ready):
        return made_by("state", OWN, state_own_kernel, [states], [keys, values], small, [ready])

    def intra(side, ready):
        outs = [
            array((half * HEAD_DIM, length), BF),
            array((3 * half, length // 2, length // 2), BF),
            part(F32),
        ]
        args = [query, keys, values]
        return made_by("intra", side, intra_kernel, outs, args, 3 * square, [ready])

    def mix(side, before, after, *sums):
        args = [query, before, made["intra", side][2], cotangent, gain, *sums]
        return made_by("mix", side, mix_kernel, [part(F32), rows], args, small, after)

    mine, theirs = carried(
        send,
        False,
        [
            state_own,
            lambda ready: intra(OWN, ready),
            lambda ready: intra(OTHER, ready),
            lambda ready, mine: mix(OWN, mine, [ready]),
        ],
    )
    before = (mine, theirs)
    _, sums = mix(OTHER, theirs, (), made["mix", OWN][1])
    heads = lax.axis_size("head")
    others = [
        lax.ppermute(sums, "head", [(i, i ^ j) for i in range(heads)]) for j in (1, 3, 2)
    ]

    def grad_args(side):
        return [made["intra", side][0], made["mix", side][0], cotangent, gain]

    gm_other, send, inverse, coef = call(
        grad_other_kernel,
        [part(BF), states, lanes, lanes],
        grad_args(OTHER) + [sums, *others],
        small,
    )

    def grad_own(ready):
        made["grad"] = call(
            grad_own_kernel,
            [part(BF), states],
            grad_args(OWN) + [inverse, coef],
            small,
            [ready],
        )
        return made["grad"]

    def back(side, ready):
        gm = gm_other if side == OTHER else made["grad"][0]
        mixture, weights = made["mix", side][0], made["intra", side][1]
        args = [query, keys, values, gm, before[side], mixture, inverse, gain, weights]
        outs = [part(BF), part(BF), part(F32), part(F32)]
        return made_by("back", side, back_kernel, outs, args, 4 * square, [ready])

    def last_own(ready, mine):
        own, other = made["back", OWN], made["back", OTHER]
        made["last"] = pl.pallas_call(
            lambda *refs: last_own_kernel(*refs[:9], *refs[10:]),
            out_shape=[part(BF), part(BF), whole, whole],
            in_specs=[VMEM] * 9 + [ANY],
            out_specs=[VMEM, VMEM, HBM, HBM],
            scratch_shapes=[dmas((4,))],
            compiler_params=pltpu.CompilerParams(vmem_limit_bytes=16 << 20),
            cost_estimate=pl.CostEstimate(
                flops=2 * small, bytes_accessed=8 * whole.size, transcendentals=0
            ),
        )(keys, values, mine, own[2], own[3], own[0], other[0], own[1], other[1], ready)
        return made["last"]

    mine, theirs = carried(
        send,
        True,
        [
            grad_own,
            lambda ready: back(OTHER, ready),
            lambda ready: back(OWN, ready),
            last_own,
        ],
    )
    gk_own, gv_own, attended, grad_q = made["last"]
    grad_k, grad_v = call(
        last_other_kernel,
        [whole, whole],
        [keys, values, theirs, *made["back", OTHER][2:], gk_own, gv_own],
        2 * small,
        out=HBM,
        scratch=halves + [dmas((2,)), dmas((2, half))],
    )
    return attended, grad_q, grad_k, grad_v


def solution(mesh):
    spec = P("ctx", "head")
    return jax.shard_map(
        body,
        mesh=mesh,
        in_specs=(spec, spec, spec, P("head"), spec),
        out_specs=(spec,) * 4,
        check_vma=False,
    )
```

```python
import functools

import jax
import jax.numpy as jnp
from jax import lax
from jax.experimental import pallas as pl
from jax.experimental.pallas import tpu as pltpu
from jax.sharding import PartitionSpec as P

HEADS = 32
HEAD_DIM = 128
EPSILON = 1e-05
BF = jnp.bfloat16
F32 = jnp.float32

X = 4
CORES = 2
PAIR = 2 * X

VMEM = pl.BlockSpec(memory_space=pltpu.VMEM)
HBM = pl.BlockSpec(memory_space=pltpu.HBM)
ANY = pl.BlockSpec(memory_space=pl.ANY)


def dot(a, b, ca, cb):
    return lax.dot_general(a, b, (((ca,), (cb,)), ((), ())), preferred_element_type=F32)


def call(kernel, outs, args, flops, after=(), ins=VMEM, out=VMEM, scratch=(), vmem=16):
    nbytes = sum(a.size * a.dtype.itemsize for a in args)
    nbytes += sum(o.size * o.dtype.itemsize for o in outs)

    ins = ins if isinstance(ins, list) else [ins] * len(args)
    out = out if isinstance(out, list) else [out] * len(outs)

    def body(*refs):
        kernel(*refs[: len(args)], *refs[len(args) + len(after) :])

    return pl.pallas_call(
        body,
        out_shape=outs,
        in_specs=ins + [ANY] * len(after),
        out_specs=out,
        scratch_shapes=list(scratch),
        compiler_params=pltpu.CompilerParams(vmem_limit_bytes=vmem << 20),
        cost_estimate=pl.CostEstimate(flops=flops, bytes_accessed=nbytes, transcendentals=0),
    )(*args, *after)


def array(shape, dtype):
    return jax.ShapeDtypeStruct(shape, dtype)


def at(h):
    return slice(h * HEAD_DIM, (h + 1) * HEAD_DIM)


def my_core():
    return lax.rem(lax.axis_index("ctx"), CORES)


def shift(i):
    return i // (2 * X * CORES)


def my_half():
    i = lax.axis_index("ctx")
    return lax.rem(i % CORES + shift(i), 2)


OWN, OTHER = 0, 1


def cols(side, j, half):
    mine = my_half()
    base = (mine if side == OWN else 1 - mine) * (half * HEAD_DIM)
    return pl.ds(pl.multiple_of(base + j * HEAD_DIM, HEAD_DIM), HEAD_DIM)


def state_own_kernel(side, a_ref, b_ref, s_ref):
    half = s_ref.shape[0] // HEAD_DIM
    for j in range(half):
        c = cols(side, j, half)
        s_ref[at(j), :] = dot(a_ref[:, c], b_ref[:, c], 0, 0)


def columns(side, half):
    mine = my_half()
    base = (mine if side == OWN else 1 - mine) * (half * HEAD_DIM)
    return pl.ds(pl.multiple_of(base, half * HEAD_DIM), half * HEAD_DIM)


def state_kernel(side, a_hbm, b_hbm, s_ref, a_ref, b_ref, sems):
    half = a_ref.shape[1] // HEAD_DIM
    copies = []
    for i, (src, dst) in enumerate(((a_hbm, a_ref), (b_hbm, b_ref))):
        copies.append(pltpu.make_async_copy(src.at[:, columns(side, half)], dst, sems.at[i]))
        copies[-1].start()
    for copy in copies:
        copy.wait()
    for j in range(half):
        s_ref[at(j), :] = dot(a_ref[:, at(j)], b_ref[:, at(j)], 0, 0)


def triangle(n, flip=False):
    rows = lax.broadcasted_iota(jnp.int32, (n, n), 0)
    cols = lax.broadcasted_iota(jnp.int32, (n, n), 1)
    return rows <= cols if flip else cols <= rows


def lower(a, b):
    n = a.shape[0] // 2
    keep = triangle(n)
    top = jnp.where(keep, dot(a[:n], b[:n], 1, 1), 0.0).astype(BF)
    left = dot(a[n:], b[:n], 1, 1).astype(BF)
    right = jnp.where(keep, dot(a[n:], b[n:], 1, 1), 0.0).astype(BF)
    return top, left, right


def lower_t(a, b):
    n = a.shape[0] // 2
    keep = triangle(n, True)
    top = jnp.where(keep, dot(b[:n], a[:n], 1, 1), 0.0).astype(BF)
    left = dot(b[:n], a[n:], 1, 1).astype(BF)
    right = jnp.where(keep, dot(b[n:], a[n:], 1, 1), 0.0).astype(BF)
    return top, left, right


def intra_kernel(side, q_ref, k_ref, v_ref, qt_ref, wt_ref, o_ref):
    n = q_ref.shape[0] // 2
    half = o_ref.shape[1] // HEAD_DIM
    for j in range(half):
        c = cols(side, j, half)
        q, k, v = q_ref[:, c], k_ref[:, c], v_ref[:, c]
        qt_ref[at(j), :] = q.T
        top, left, right = lower(q, k)
        o_ref[:n, at(j)] = dot(top, v[:n], 1, 0)
        o_ref[n:, at(j)] = dot(left, v[:n], 1, 0) + dot(right, v[n:], 1, 0)
        for i, block in enumerate(lower_t(q, k)):
            wt_ref[3 * j + i] = block


def mix_kernel(side, q_ref, s_ref, i_ref, c_ref, g_ref, *refs):
    before_ref = refs[0] if side == OTHER else None
    m_ref, p_ref = refs[-2:]
    half = m_ref.shape[1] // HEAD_DIM
    state = [s_ref[at(j), :].astype(BF) for j in range(half)]
    for i in range(q_ref.shape[0] // 128):
        rows = slice(i * 128, (i + 1) * 128)
        squares = jnp.zeros((128, HEAD_DIM), F32)
        products = jnp.zeros((128, HEAD_DIM), F32)
        for j in range(half):
            c = cols(side, j, half)
            m = i_ref[rows, at(j)] + dot(q_ref[rows, c], state[j], 1, 0)
            m_ref[rows, at(j)] = m
            squares = squares + m * m
            products = products + (c_ref[rows, c].astype(F32) * g_ref[:, c]) * m
        for row, value in ((i, squares), (4 + i, products)):
            value = jnp.sum(value.T, axis=0, keepdims=True)
            if side == OTHER:
                value = value + before_ref[row : row + 1, :]
            p_ref[row : row + 1, :] = value


def spread(row):
    return jnp.broadcast_to(row, (128, 128)).T


def grad(side, qt_ref, m_ref, c_ref, g_ref, inv_ref, cf_ref, gm_ref, s_ref):
    half = m_ref.shape[1] // HEAD_DIM
    for j in range(half):
        c = cols(side, j, half)
        scaled = c_ref[:, c].astype(F32) * g_ref[:, c]
        gm = (inv_ref[...] * scaled - m_ref[:, at(j)] * cf_ref[...]).astype(BF)
        gm_ref[:, at(j)] = gm
        s_ref[at(j), :] = dot(qt_ref[at(j), :], gm, 1, 0)


def grad_other_kernel(qt_ref, m_ref, c_ref, g_ref, p0, p1, p2, p3, gm_ref, s_ref, inv_ref, cf_ref):
    width = HEADS * HEAD_DIM
    sums = p0[...] + p1[...] + p2[...] + p3[...]
    inverse = lax.rsqrt(sums[:4] / width + EPSILON)
    coef = inverse * inverse * inverse * sums[4:] / width
    for i in range(4):
        rows = slice(i * 128, (i + 1) * 128)
        inv_ref[rows, :] = spread(inverse[i : i + 1])
        cf_ref[rows, :] = spread(coef[i : i + 1])
    grad(OTHER, qt_ref, m_ref, c_ref, g_ref, inv_ref, cf_ref, gm_ref, s_ref)


def grad_own_kernel(qt_ref, m_ref, c_ref, g_ref, inv_ref, cf_ref, gm_ref, s_ref):
    grad(OWN, qt_ref, m_ref, c_ref, g_ref, inv_ref, cf_ref, gm_ref, s_ref)


def back(
    side, q_ref, k_ref, v_ref, gm_ref, s_ref, m_ref, inv_ref, g_ref, wt_ref,
    at_ref, gq_ref, gk_ref, gv_ref, then=lambda j: None,
):
    n = q_ref.shape[0] // 2
    half = gm_ref.shape[1] // HEAD_DIM
    for j in range(half):
        c = cols(side, j, half)
        at_ref[:, at(j)] = (m_ref[:, at(j)] * inv_ref[...] * g_ref[:, c]).astype(BF)
        q, k, v, gm = q_ref[:, c], k_ref[:, c], v_ref[:, c], gm_ref[:, at(j)]
        top, left, right = lower(gm, v)
        s = s_ref[at(j), :].astype(BF)
        gq_ref[:n, at(j)] = (dot(top, k[:n], 1, 0) + dot(gm[:n], s, 1, 1)).astype(BF)
        gq_ref[n:, at(j)] = (
            dot(left, k[:n], 1, 0) + dot(right, k[n:], 1, 0) + dot(gm[n:], s, 1, 1)
        ).astype(BF)
        gk_ref[:n, at(j)] = dot(top, q[:n], 0, 0) + dot(left, q[n:], 0, 0)
        gk_ref[n:, at(j)] = dot(right, q[n:], 0, 0)
        top, left, right = wt_ref[3 * j], wt_ref[3 * j + 1], wt_ref[3 * j + 2]
        gv_ref[:n, at(j)] = dot(top, gm[:n], 1, 0) + dot(left, gm[n:], 1, 0)
        gv_ref[n:, at(j)] = dot(right, gm[n:], 1, 0)
        then(j)


def send_out(pairs, half, sems):
    copies = []
    for i, (side, src, dst) in enumerate(pairs):
        copies.append(pltpu.make_async_copy(src, dst.at[:, columns(side, half)], sems.at[i]))
        copies[-1].start()
    return copies


def send_heads(j, half, side, pairs, sems):
    copies = []
    for i, (src, dst) in enumerate(pairs):
        copies.append(
            pltpu.make_async_copy(src.at[:, at(j)], dst.at[:, cols(side, j, half)], sems.at[i, j])
        )
        copies[-1].start()
    return copies


def back_other_kernel(*refs):
    back(OTHER, *refs)


def back_own_kernel(*refs):
    ins, (at_other, gq_other) = refs[:9], refs[9:11]
    gk_ref, gv_ref, at_hbm, gq_hbm, at_ref, gq_ref, sems, head_sems = refs[11:]
    half = gk_ref.shape[1] // HEAD_DIM
    copies = send_out([(OTHER, at_other, at_hbm), (OTHER, gq_other, gq_hbm)], half, sems)
    pairs = ((at_ref, at_hbm), (gq_ref, gq_hbm))

    def then(j):
        copies.extend(send_heads(j, half, OWN, pairs, head_sems))

    back(OWN, *ins, at_ref, gq_ref, gk_ref, gv_ref, then)
    for copy in copies:
        copy.wait()


def last(side, k_ref, v_ref, s_ref, gki_ref, gvi_ref, gk_ref, gv_ref, then=lambda j: None):
    half = gki_ref.shape[1] // HEAD_DIM
    for j in range(half):
        c = cols(side, j, half)
        s = s_ref[at(j), :].astype(BF)
        gk_ref[:, at(j)] = (gki_ref[:, at(j)] + dot(v_ref[:, c], s, 1, 1)).astype(BF)
        gv_ref[:, at(j)] = (gvi_ref[:, at(j)] + dot(k_ref[:, c], s, 1, 0)).astype(BF)
        then(j)


def last_own_kernel(*refs):
    last(OWN, *refs)


def last_other_kernel(
    k_ref, v_ref, s_ref, gki_ref, gvi_ref, gko_ref, gvo_ref,
    gk_hbm, gv_hbm, gk_ref, gv_ref, sems, head_sems,
):
    half = gki_ref.shape[1] // HEAD_DIM
    copies = send_out([(OWN, gko_ref, gk_hbm), (OWN, gvo_ref, gv_hbm)], half, sems)
    pairs = ((gk_ref, gk_hbm), (gv_ref, gv_hbm))

    def then(j):
        copies.extend(send_heads(j, half, OTHER, pairs, head_sems))

    last(OTHER, k_ref, v_ref, s_ref, gki_ref, gvi_ref, gk_ref, gv_ref, then)
    for copy in copies:
        copy.wait()


def add_kernel(a_ref, b_ref, o_ref):
    o_ref[...] = (a_ref[...] + b_ref[...]).reshape(o_ref.shape)


def finish_kernel(reverse, g_ref, keep_ref, other_ref, mine_ref, give_ref):
    first = g_ref[...].reshape(keep_ref.shape)
    leads = my_core() == (1 if reverse else 0)
    second = first + jnp.where(leads, keep_ref[...], other_ref[...])
    mine_ref[...] = jnp.where(leads, first, second)
    give_ref[...] = jnp.where(leads, second, first)


def running_kernel(reverse, g_ref, o_ref, t_ref):
    total = jnp.zeros(g_ref.shape[1:], F32)
    for i in range(g_ref.shape[0]) if not reverse else reversed(range(g_ref.shape[0])):
        o_ref[i] = total
        total = total + g_ref[i]
    t_ref[...] = total


def outer_kernel(reverse, g_ref, near_ref, far_ref, o_ref):
    z = lax.axis_index("ctx") // (X * CORES)
    bit = 0 if reverse else 1
    near, far = lax.rem(z // 2, 2) == bit, z // 4 == bit
    total = jnp.where(near, near_ref[...], 0.0) + jnp.where(far, far_ref[...], 0.0)
    for i in range(g_ref.shape[0]):
        o_ref[i] = g_ref[i] + total


def carried(send, reverse, windows):
    count = lax.axis_size("ctx")
    pieces_of = (PAIR, send.shape[0] // PAIR, HEAD_DIM)
    swap = [(i, i ^ 1) for i in range(count)]
    def on(chip, half):
        return chip * CORES + (half + shift(chip * CORES)) % CORES

    groups = [
        [on(pair * PAIR + i, half) for i in range(PAIR)]
        for pair in range(count // (PAIR * CORES))
        for half in range(2)
    ]
    across = (6, 7, 4, 5, 2, 3, 0, 1)

    def partners(of):
        chips = [(z * X + x, of(z) * X + x) for z in range(len(across)) for x in range(X)]
        return [(on(a, half), on(b, half)) for a, b in chips for half in range(2)]

    near_z = partners(lambda z: z ^ 2)
    far_z = partners(lambda z: across[z])

    def add(a, b, after, shape):
        return call(add_kernel, [array(shape, F32)], [a, b], a.size, after, vmem=4)[0]

    other = lax.ppermute(send, "ctx", swap)
    keep = windows[0](send)[-1]
    pieces = add(keep, other, (), pieces_of)
    pieces = lax.all_to_all(pieces, "ctx", 0, 0, axis_index_groups=groups)
    inner, total = call(
        functools.partial(running_kernel, reverse),
        [array(pieces.shape, F32), array(pieces.shape[1:], F32)],
        [pieces],
        pieces.size,
        vmem=4,
    )
    near = lax.ppermute(total, "ctx", near_z)
    after = windows[1](total)[-1:]
    total = add(total, near, after, total.shape)
    far = lax.ppermute(total, "ctx", far_z)
    after = windows[2](total)[-1:]
    (pieces,) = call(
        functools.partial(outer_kernel, reverse),
        [array(pieces.shape, F32)],
        [inner, near, far],
        pieces.size,
        after,
        vmem=4,
    )
    pieces = lax.all_to_all(pieces, "ctx", 0, 0, axis_index_groups=groups)
    mine, give = call(
        functools.partial(finish_kernel, reverse),
        [array(send.shape, F32)] * 2,
        [pieces, keep, other],
        pieces.size,
        vmem=4,
    )
    theirs = lax.ppermute(give, "ctx", swap)
    windows[3](give, mine)
    return mine, theirs


def body(query, keys, values, gain, cotangent):
    length, width = query.shape
    half = width // HEAD_DIM // 2
    square = 2 * length * length * HEAD_DIM * half
    small = 2 * length * HEAD_DIM * HEAD_DIM * half
    gain = gain.reshape(1, width)
    whole = array((length, width), BF)
    part = lambda dtype: array((length, half * HEAD_DIM), dtype)
    states = array((half * HEAD_DIM, HEAD_DIM), F32)
    lanes = array((length, HEAD_DIM), F32)
    rows = array((8, 128), F32)
    dmas = pltpu.SemaphoreType.DMA
    halves = [pltpu.VMEM((length, half * HEAD_DIM), BF)] * 2
    made = {}

    def made_by(name, side, kernel, outs, args, flops, after=(), **options):
        made[name, side] = call(functools.partial(kernel, side), outs, args, flops, after, **options)
        return made[name, side]

    in_hbm = [pltpu.with_memory_space_constraint(a, pltpu.HBM) for a in (keys, values)]

    (send,) = made_by(
        "state", OTHER, state_kernel, [states], in_hbm, small,
        ins=HBM, scratch=halves + [dmas((2,))],
    )

    def state_own(ready):
        return made_by("state", OWN, state_own_kernel, [states], [keys, values], small, [ready])

    def intra(side, ready):
        outs = [
            array((half * HEAD_DIM, length), BF),
            array((3 * half, length // 2, length // 2), BF),
            part(F32),
        ]
        args = [query, keys, values]
        return made_by("intra", side, intra_kernel, outs, args, 3 * square, [ready])

    def mix(side, before, after, *sums):
        args = [query, before, made["intra", side][2], cotangent, gain, *sums]
        return made_by("mix", side, mix_kernel, [part(F32), rows], args, small, after)

    mine, theirs = carried(
        send,
        False,
        [
            state_own,
            lambda ready: intra(OWN, ready),
            lambda ready: intra(OTHER, ready),
            lambda ready, mine: mix(OWN, mine, [ready]),
        ],
    )
    before = (mine, theirs)
    _, sums = mix(OTHER, theirs, (), made["mix", OWN][1])
    heads = lax.axis_size("head")
    others = [
        lax.ppermute(sums, "head", [(i, i ^ j) for i in range(heads)]) for j in (1, 3, 2)
    ]

    def grad_args(side):
        return [made["intra", side][0], made["mix", side][0], cotangent, gain]

    gm_other, send, inverse, coef = call(
        grad_other_kernel,
        [part(BF), states, lanes, lanes],
        grad_args(OTHER) + [sums, *others],
        small,
    )

    def grad_own(ready):
        made["grad"] = call(
            grad_own_kernel,
            [part(BF), states],
            grad_args(OWN) + [inverse, coef],
            small,
            [ready],
        )
        return made["grad"]

    def back_args(side):
        gm = gm_other if side == OTHER else made["grad"][0]
        mixture, weights = made["mix", side][0], made["intra", side][1]
        return [query, keys, values, gm, before[side], mixture, inverse, gain, weights]

    def back_other(ready):
        outs = [part(BF), part(BF), part(F32), part(F32)]
        made["back"] = call(back_other_kernel, outs, back_args(OTHER), 4 * square, [ready])
        return made["back"]

    def back_own(ready):
        *made["rows"], gk, gv = call(
            lambda *refs: back_own_kernel(*refs[:11], *refs[13:15], *refs[11:13], *refs[15:]),
            [whole, whole, part(F32), part(F32)],
            [*back_args(OWN), *made["back"][:2]],
            4 * square,
            [ready],
            out=[HBM, HBM, VMEM, VMEM],
            scratch=halves + [dmas((2,)), dmas((2, half))],
        )
        made["own"] = [gk, gv]
        return made["own"]

    def last_own(ready, mine):
        args = [keys, values, mine, *made["own"]]
        made["last"] = call(last_own_kernel, [part(BF), part(BF)], args, 2 * small, [ready])
        return made["last"]

    _, theirs = carried(send, True, [grad_own, back_other, back_own, last_own])
    grads = call(
        last_other_kernel,
        [whole, whole],
        [keys, values, theirs, *made["back"][2:], *made["last"]],
        2 * small,
        out=HBM,
        scratch=halves + [dmas((2,)), dmas((2, half))],
    )
    return (*made["rows"], *grads)


def solution(mesh):
    spec = P("ctx", "head")
    return jax.shard_map(
        body,
        mesh=mesh,
        in_specs=(spec, spec, spec, P("head"), spec),
        out_specs=(spec,) * 4,
        check_vma=False,
    )
```

```python
import functools

import jax
import jax.numpy as jnp
from jax import lax
from jax.experimental import pallas as pl
from jax.experimental.pallas import tpu as pltpu
from jax.sharding import PartitionSpec as P

HEADS = 32
HEAD_DIM = 128
EPSILON = 1e-05
BF = jnp.bfloat16
F32 = jnp.float32

X = 4
CORES = 2
PAIR = 2 * X

VMEM = pl.BlockSpec(memory_space=pltpu.VMEM)
HBM = pl.BlockSpec(memory_space=pltpu.HBM)
ANY = pl.BlockSpec(memory_space=pl.ANY)


def dot(a, b, ca, cb):
    return lax.dot_general(a, b, (((ca,), (cb,)), ((), ())), preferred_element_type=F32)


def call(kernel, outs, args, flops, after=(), ins=VMEM, out=VMEM, scratch=(), vmem=16):
    nbytes = sum(a.size * a.dtype.itemsize for a in args)
    nbytes += sum(o.size * o.dtype.itemsize for o in outs)

    ins = ins if isinstance(ins, list) else [ins] * len(args)
    out = out if isinstance(out, list) else [out] * len(outs)

    def body(*refs):
        kernel(*refs[: len(args)], *refs[len(args) + len(after) :])

    return pl.pallas_call(
        body,
        out_shape=outs,
        in_specs=ins + [ANY] * len(after),
        out_specs=out,
        scratch_shapes=list(scratch),
        compiler_params=pltpu.CompilerParams(vmem_limit_bytes=vmem << 20),
        cost_estimate=pl.CostEstimate(flops=flops, bytes_accessed=nbytes, transcendentals=0),
    )(*args, *after)


def array(shape, dtype):
    return jax.ShapeDtypeStruct(shape, dtype)


def at(h):
    return slice(h * HEAD_DIM, (h + 1) * HEAD_DIM)


def my_core():
    return lax.rem(lax.axis_index("ctx"), CORES)


def shift(i):
    return i // (2 * X * CORES)


def my_half():
    i = lax.axis_index("ctx")
    return lax.rem(i % CORES + shift(i), 2)


OWN, OTHER = 0, 1
FIRST = ((0, 1), (1, 3))


def cols(side, j, half):
    mine = my_half()
    base = (mine if side == OWN else 1 - mine) * (half * HEAD_DIM)
    return pl.ds(pl.multiple_of(base + j * HEAD_DIM, HEAD_DIM), HEAD_DIM)


def state_own_kernel(side, a_ref, b_ref, s_ref):
    half = s_ref.shape[0] // HEAD_DIM
    for j in range(half):
        c = cols(side, j, half)
        s_ref[at(j), :] = dot(a_ref[:, c], b_ref[:, c], 0, 0)


def columns(side, half):
    mine = my_half()
    base = (mine if side == OWN else 1 - mine) * (half * HEAD_DIM)
    return pl.ds(pl.multiple_of(base, half * HEAD_DIM), half * HEAD_DIM)


def state_kernel(side, a_hbm, b_hbm, s_ref, a_ref, b_ref, sems):
    half = a_ref.shape[1] // HEAD_DIM
    copies = []
    for i, (src, dst) in enumerate(((a_hbm, a_ref), (b_hbm, b_ref))):
        copies.append(pltpu.make_async_copy(src.at[:, columns(side, half)], dst, sems.at[i]))
        copies[-1].start()
    for copy in copies:
        copy.wait()
    for j in range(half):
        s_ref[at(j), :] = dot(a_ref[:, at(j)], b_ref[:, at(j)], 0, 0)


def triangle(n, flip=False):
    rows = lax.broadcasted_iota(jnp.int32, (n, n), 0)
    cols = lax.broadcasted_iota(jnp.int32, (n, n), 1)
    return rows <= cols if flip else cols <= rows


def lower(a, b):
    n = a.shape[0] // 2
    keep = triangle(n)
    top = jnp.where(keep, dot(a[:n], b[:n], 1, 1), 0.0).astype(BF)
    left = dot(a[n:], b[:n], 1, 1).astype(BF)
    right = jnp.where(keep, dot(a[n:], b[n:], 1, 1), 0.0).astype(BF)
    return top, left, right


def lower_t(a, b):
    n = a.shape[0] // 2
    keep = triangle(n, True)
    top = jnp.where(keep, dot(b[:n], a[:n], 1, 1), 0.0).astype(BF)
    left = dot(b[:n], a[n:], 1, 1).astype(BF)
    right = jnp.where(keep, dot(b[n:], a[n:], 1, 1), 0.0).astype(BF)
    return top, left, right


def intra_kernel(side, q_ref, k_ref, v_ref, qt_ref, o_ref):
    n = q_ref.shape[0] // 2
    half = o_ref.shape[1] // HEAD_DIM
    for j in range(half):
        c = cols(side, j, half)
        q, k, v = q_ref[:, c], k_ref[:, c], v_ref[:, c]
        qt_ref[at(j), :] = q.T
        top, left, right = lower(q, k)
        o_ref[:n, at(j)] = dot(top, v[:n], 1, 0)
        o_ref[n:, at(j)] = dot(left, v[:n], 1, 0) + dot(right, v[n:], 1, 0)


def weights_kernel(q_ref, k_ref, own_ref, other_ref):
    half = own_ref.shape[0] // 3
    for side, wt_ref in ((OWN, own_ref), (OTHER, other_ref)):
        for j in range(half):
            c = cols(side, j, half)
            for i, block in enumerate(lower_t(q_ref[:, c], k_ref[:, c])):
                wt_ref[3 * j + i] = block


def mix_kernel(side, q_ref, s_ref, i_ref, c_ref, g_ref, *refs):
    before_ref = refs[0] if side == OTHER else None
    m_ref, p_ref = refs[-2:]
    half = m_ref.shape[1] // HEAD_DIM
    state = [s_ref[at(j), :].astype(BF) for j in range(half)]
    for i in range(q_ref.shape[0] // 128):
        rows = slice(i * 128, (i + 1) * 128)
        squares = jnp.zeros((128, HEAD_DIM), F32)
        products = jnp.zeros((128, HEAD_DIM), F32)
        for j in range(half):
            c = cols(side, j, half)
            m = i_ref[rows, at(j)] + dot(q_ref[rows, c], state[j], 1, 0)
            m_ref[rows, at(j)] = m
            squares = squares + m * m
            products = products + (c_ref[rows, c].astype(F32) * g_ref[:, c]) * m
        for row, value in ((i, squares), (4 + i, products)):
            value = jnp.sum(value.T, axis=0, keepdims=True)
            if side == OTHER:
                value = value + before_ref[row : row + 1, :]
            p_ref[row : row + 1, :] = value


def spread(row):
    return jnp.broadcast_to(row, (128, 128)).T


def grad(side, qt_ref, m_ref, c_ref, g_ref, inv_ref, cf_ref, gm_ref, s_ref):
    half = m_ref.shape[1] // HEAD_DIM
    for j in range(half):
        c = cols(side, j, half)
        scaled = c_ref[:, c].astype(F32) * g_ref[:, c]
        gm = (inv_ref[...] * scaled - m_ref[:, at(j)] * cf_ref[...]).astype(BF)
        gm_ref[:, at(j)] = gm
        s_ref[at(j), :] = dot(qt_ref[at(j), :], gm, 1, 0)


def grad_other_kernel(qt_ref, m_ref, c_ref, g_ref, p0, p1, p2, p3, gm_ref, s_ref, inv_ref, cf_ref):
    width = HEADS * HEAD_DIM
    sums = p0[...] + p1[...] + p2[...] + p3[...]
    inverse = lax.rsqrt(sums[:4] / width + EPSILON)
    coef = inverse * inverse * inverse * sums[4:] / width
    for i in range(4):
        rows = slice(i * 128, (i + 1) * 128)
        inv_ref[rows, :] = spread(inverse[i : i + 1])
        cf_ref[rows, :] = spread(coef[i : i + 1])
    grad(OTHER, qt_ref, m_ref, c_ref, g_ref, inv_ref, cf_ref, gm_ref, s_ref)


def grad_own_kernel(qt_ref, m_ref, c_ref, g_ref, inv_ref, cf_ref, gm_ref, s_ref):
    grad(OWN, qt_ref, m_ref, c_ref, g_ref, inv_ref, cf_ref, gm_ref, s_ref)


def back(
    side, heads, q_ref, k_ref, v_ref, gm_ref, s_ref, m_ref, inv_ref, g_ref, wt_ref,
    at_ref, gq_ref, gk_ref, gv_ref, then=lambda j: None,
):
    n = q_ref.shape[0] // 2
    half = gm_ref.shape[1] // HEAD_DIM
    for i, j in enumerate(heads):
        c = cols(side, j, half)
        at_ref[:, at(i)] = (m_ref[:, at(j)] * inv_ref[...] * g_ref[:, c]).astype(BF)
        q, k, v, gm = q_ref[:, c], k_ref[:, c], v_ref[:, c], gm_ref[:, at(j)]
        top, left, right = lower(gm, v)
        s = s_ref[at(j), :].astype(BF)
        gq_ref[:n, at(i)] = (dot(top, k[:n], 1, 0) + dot(gm[:n], s, 1, 1)).astype(BF)
        gq_ref[n:, at(i)] = (
            dot(left, k[:n], 1, 0) + dot(right, k[n:], 1, 0) + dot(gm[n:], s, 1, 1)
        ).astype(BF)
        gk_ref[:n, at(i)] = dot(top, q[:n], 0, 0) + dot(left, q[n:], 0, 0)
        gk_ref[n:, at(i)] = dot(right, q[n:], 0, 0)
        top, left, right = wt_ref[3 * j], wt_ref[3 * j + 1], wt_ref[3 * j + 2]
        gv_ref[:n, at(i)] = dot(top, gm[:n], 1, 0) + dot(left, gm[n:], 1, 0)
        gv_ref[n:, at(i)] = dot(right, gm[n:], 1, 0)
        then(j)


def send_out(pairs, half, sems):
    copies = []
    for i, (side, src, dst) in enumerate(pairs):
        copies.append(pltpu.make_async_copy(src, dst.at[:, columns(side, half)], sems.at[i]))
        copies[-1].start()
    return copies


def send_two(j, half, pairs, sems):
    copies = []
    if j % 2:
        base = cols(OTHER, j - 1, half).start
        c = pl.ds(pl.multiple_of(base, 2 * HEAD_DIM), 2 * HEAD_DIM)
        here = slice((j - 1) * HEAD_DIM, (j + 1) * HEAD_DIM)
        for i, (src, dst) in enumerate(pairs):
            copies.append(pltpu.make_async_copy(src.at[:, here], dst.at[:, c], sems.at[i, j]))
            copies[-1].start()
    return copies


def send_heads(j, half, side, pairs, sems):
    copies = []
    for i, (src, dst) in enumerate(pairs):
        copies.append(
            pltpu.make_async_copy(src.at[:, at(j)], dst.at[:, cols(side, j, half)], sems.at[i, j])
        )
        copies[-1].start()
    return copies


def back_other_kernel(heads, *refs):
    back(OTHER, heads, *refs)


def back_own_kernel(*refs):
    ins, others = refs[:9], refs[9:13]
    gk_ref, gv_ref, at_hbm, gq_hbm, at_ref, gq_ref, sems, head_sems = refs[13:]
    half = gk_ref.shape[1] // HEAD_DIM
    copies = []
    for i, src in enumerate(others):
        first, count = FIRST[i // 2]
        base = cols(OTHER, first, half).start
        dst = (at_hbm, gq_hbm)[i % 2].at[:, pl.ds(pl.multiple_of(base, HEAD_DIM), count * HEAD_DIM)]
        copies.append(pltpu.make_async_copy(src, dst, sems.at[i]))
        copies[-1].start()
    pairs = ((at_ref, at_hbm), (gq_ref, gq_hbm))

    def then(j):
        copies.extend(send_heads(j, half, OWN, pairs, head_sems))

    back(OWN, range(half), *ins, at_ref, gq_ref, gk_ref, gv_ref, then)
    for copy in copies:
        copy.wait()


def last(side, k_ref, v_ref, s_ref, inner, gk_ref, gv_ref, then=lambda j: None):
    half = gk_ref.shape[1] // HEAD_DIM
    pieces = [(*refs, i) for refs in inner for i in range(refs[0].shape[1] // HEAD_DIM)]
    for j, (gki_ref, gvi_ref, i) in enumerate(pieces):
        c = cols(side, j, half)
        s = s_ref[at(j), :].astype(BF)
        gk_ref[:, at(j)] = (gki_ref[:, at(i)] + dot(v_ref[:, c], s, 1, 1)).astype(BF)
        gv_ref[:, at(j)] = (gvi_ref[:, at(i)] + dot(k_ref[:, c], s, 1, 0)).astype(BF)
        then(j)


def last_own_kernel(k_ref, v_ref, s_ref, gki_ref, gvi_ref, gk_ref, gv_ref):
    last(OWN, k_ref, v_ref, s_ref, ((gki_ref, gvi_ref),), gk_ref, gv_ref)


def last_other_kernel(
    k_ref, v_ref, s_ref, gka_ref, gva_ref, gkb_ref, gvb_ref, gko_ref, gvo_ref,
    gk_hbm, gv_hbm, gk_ref, gv_ref, sems, head_sems,
):
    half = gk_ref.shape[1] // HEAD_DIM
    inner = ((gka_ref, gva_ref), (gkb_ref, gvb_ref))
    copies = send_out([(OWN, gko_ref, gk_hbm), (OWN, gvo_ref, gv_hbm)], half, sems)
    pairs = ((gk_ref, gk_hbm), (gv_ref, gv_hbm))

    def then(j):
        copies.extend(send_two(j, half, pairs, head_sems))

    last(OTHER, k_ref, v_ref, s_ref, inner, gk_ref, gv_ref, then)
    for copy in copies:
        copy.wait()


def add_kernel(a_ref, b_ref, o_ref):
    o_ref[...] = (a_ref[...] + b_ref[...]).reshape(o_ref.shape)


def finish_kernel(reverse, g_ref, keep_ref, other_ref, mine_ref, give_ref):
    first = g_ref[...].reshape(keep_ref.shape)
    leads = my_core() == (1 if reverse else 0)
    second = first + jnp.where(leads, keep_ref[...], other_ref[...])
    mine_ref[...] = jnp.where(leads, first, second)
    give_ref[...] = jnp.where(leads, second, first)


def running_kernel(reverse, g_ref, o_ref, t_ref):
    total = jnp.zeros(g_ref.shape[1:], F32)
    for i in range(g_ref.shape[0]) if not reverse else reversed(range(g_ref.shape[0])):
        o_ref[i] = total
        total = total + g_ref[i]
    t_ref[...] = total


def rank(reverse):
    pair = lax.axis_index("ctx") // (2 * X * CORES)
    return 3 - pair if reverse else pair


def middle_kernel(reverse, t_ref, far_ref, o_ref):
    place = rank(reverse)
    own = jnp.where(place == 3, 0.0, t_ref[...])
    o_ref[...] = own + jnp.where(place >= 2, far_ref[...], 0.0)


def outer_kernel(reverse, g_ref, far_ref, near_ref, o_ref):
    place = rank(reverse)
    total = jnp.where(place >= 2, far_ref[...], 0.0) + jnp.where(place >= 1, near_ref[...], 0.0)
    for i in range(g_ref.shape[0]):
        o_ref[i] = g_ref[i] + total


def carried(send, reverse, windows):
    count = lax.axis_size("ctx")
    pieces_of = (PAIR, send.shape[0] // PAIR, HEAD_DIM)
    swap = [(i, i ^ 1) for i in range(count)]
    def on(chip, half):
        return chip * CORES + (half + shift(chip * CORES)) % CORES

    groups = [
        [on(pair * PAIR + i, half) for i in range(PAIR)]
        for pair in range(count // (PAIR * CORES))
        for half in range(2)
    ]
    across = (6, 7, 4, 5, 2, 3, 0, 1)

    def partners(of):
        chips = [(z * X + x, of(z) * X + x) for z in range(len(across)) for x in range(X)]
        return [(on(a, half), on(b, half)) for a, b in chips for half in range(2)]

    near_z = partners(lambda z: z ^ 2)
    far_z = partners(lambda z: across[z])

    def add(a, b, after, shape):
        return call(add_kernel, [array(shape, F32)], [a, b], a.size, after, vmem=4)[0]

    other = lax.ppermute(send, "ctx", swap)
    keep = windows[0](send)[-1]
    pieces = add(keep, other, (), pieces_of)
    pieces = lax.all_to_all(pieces, "ctx", 0, 0, axis_index_groups=groups)
    inner, total = call(
        functools.partial(running_kernel, reverse),
        [array(pieces.shape, F32), array(pieces.shape[1:], F32)],
        [pieces],
        pieces.size,
        vmem=4,
    )
    far = lax.ppermute(total, "ctx", far_z)
    after = windows[1](total)[-1:]
    (total,) = call(
        functools.partial(middle_kernel, reverse),
        [array(total.shape, F32)],
        [total, far],
        total.size,
        after,
        vmem=4,
    )
    near = lax.ppermute(total, "ctx", near_z)
    after = windows[2](total)[-1:]
    (pieces,) = call(
        functools.partial(outer_kernel, reverse),
        [array(pieces.shape, F32)],
        [inner, far, near],
        pieces.size,
        after,
        vmem=4,
    )
    pieces = lax.all_to_all(pieces, "ctx", 0, 0, axis_index_groups=groups)
    mine, give = call(
        functools.partial(finish_kernel, reverse),
        [array(send.shape, F32)] * 2,
        [pieces, keep, other],
        pieces.size,
        vmem=4,
    )
    theirs = lax.ppermute(give, "ctx", swap)
    windows[3](give, mine)
    return mine, theirs


def body(query, keys, values, gain, cotangent):
    length, width = query.shape
    half = width // HEAD_DIM // 2
    square = 2 * length * length * HEAD_DIM * half
    small = 2 * length * HEAD_DIM * HEAD_DIM * half
    gain = gain.reshape(1, width)
    whole = array((length, width), BF)
    part = lambda dtype: array((length, half * HEAD_DIM), dtype)
    states = array((half * HEAD_DIM, HEAD_DIM), F32)
    lanes = array((length, HEAD_DIM), F32)
    rows = array((8, 128), F32)
    dmas = pltpu.SemaphoreType.DMA
    halves = [pltpu.VMEM((length, half * HEAD_DIM), BF)] * 2
    made = {}

    def made_by(name, side, kernel, outs, args, flops, after=(), **options):
        made[name, side] = call(functools.partial(kernel, side), outs, args, flops, after, **options)
        return made[name, side]

    in_hbm = [pltpu.with_memory_space_constraint(a, pltpu.HBM) for a in (keys, values)]

    (send,) = made_by(
        "state", OTHER, state_kernel, [states], in_hbm, small,
        ins=HBM, scratch=halves + [dmas((2,))],
    )

    def state_own(ready):
        return made_by("state", OWN, state_own_kernel, [states], [keys, values], small, [ready])

    def intra(side, ready):
        outs = [
            array((half * HEAD_DIM, length), BF),
            part(F32),
        ]
        args = [query, keys, values]
        return made_by("intra", side, intra_kernel, outs, args, 3 * square, [ready])

    def mix(side, before, after, *sums):
        args = [query, before, made["intra", side][1], cotangent, gain, *sums]
        return made_by("mix", side, mix_kernel, [part(F32), rows], args, small, after)

    mine, theirs = carried(
        send,
        False,
        [
            state_own,
            lambda ready: intra(OWN, ready),
            lambda ready: intra(OTHER, ready),
            lambda ready, mine: mix(OWN, mine, [ready]),
        ],
    )
    before = (mine, theirs)
    _, sums = mix(OTHER, theirs, (), made["mix", OWN][1])
    heads = lax.axis_size("head")
    places = range(lax.axis_size("ctx"))

    def turn(first, second):
        by = (first, second)
        return [
            (i * heads + j, i * heads + (j ^ by[i % CORES])) for i in places for j in range(heads)
        ]

    others = [
        lax.ppermute(sums, ("ctx", "head"), turn(*by)) for by in zip((1, 3, 2), (3, 2, 1))
    ]

    weights_t = call(
        weights_kernel,
        [array((3 * half, length // 2, length // 2), BF)] * 2,
        [query, keys],
        2 * square,
        [sums],
    )

    def grad_args(side):
        return [made["intra", side][0], made["mix", side][0], cotangent, gain]

    gm_other, send, inverse, coef = call(
        grad_other_kernel,
        [part(BF), states, lanes, lanes],
        grad_args(OTHER) + [sums, *others],
        small,
        weights_t[:1],
    )

    def grad_own(ready):
        made["grad"] = call(
            grad_own_kernel,
            [part(BF), states],
            grad_args(OWN) + [inverse, coef],
            small,
            [ready],
        )
        return made["grad"]

    def back_args(side):
        gm = gm_other if side == OTHER else made["grad"][0]
        mixture, weights = made["mix", side][0], weights_t[side]
        return [query, keys, values, gm, before[side], mixture, inverse, gain, weights]

    made["back"] = []

    def back_other(ready):
        first, count = FIRST[len(made["back"])]
        piece = lambda dtype: array((length, count * HEAD_DIM), dtype)
        made["back"].append(
            call(
                functools.partial(back_other_kernel, range(first, first + count)),
                [piece(BF), piece(BF), piece(F32), piece(F32)],
                back_args(OTHER),
                square * count,
                [ready],
            )
        )
        return made["back"][-1]

    def grad_and_back(ready):
        back_piece = back_other(ready)
        return [*back_piece, *grad_own(back_piece[-1])]

    def back_own(ready):
        *made["rows"], gk, gv = call(
            lambda *refs: back_own_kernel(*refs[:13], *refs[15:17], *refs[13:15], *refs[17:]),
            [whole, whole, part(F32), part(F32)],
            [*back_args(OWN), *made["back"][0][:2], *made["back"][1][:2]],
            4 * square,
            [ready],
            out=[HBM, HBM, VMEM, VMEM],
            scratch=halves + [dmas((4,)), dmas((2, half))],
        )
        made["own"] = [gk, gv]
        return made["own"]

    def last_own(ready, mine):
        args = [keys, values, mine, *made["own"]]
        made["last"] = call(last_own_kernel, [part(BF), part(BF)], args, 2 * small, [ready])
        return made["last"]

    _, theirs = carried(send, True, [grad_and_back, back_other, back_own, last_own])
    grads = call(
        last_other_kernel,
        [whole, whole],
        [keys, values, theirs, *made["back"][0][2:], *made["back"][1][2:], *made["last"]],
        2 * small,
        out=HBM,
        scratch=halves + [dmas((2,)), dmas((2, half))],
    )
    return (*made["rows"], *grads)


def solution(mesh):
    spec = P("ctx", "head")
    return jax.shard_map(
        body,
        mesh=mesh,
        in_specs=(spec, spec, spec, P("head"), spec),
        out_specs=(spec,) * 4,
        check_vma=False,
    )
```

```python
import functools

import jax
import jax.numpy as jnp
from jax import lax
from jax.experimental import pallas as pl
from jax.experimental.pallas import tpu as pltpu
from jax.sharding import PartitionSpec as P

HEADS = 32
HEAD_DIM = 128
EPSILON = 1e-05
BF = jnp.bfloat16
F32 = jnp.float32

X = 4
CORES = 2
PAIR = 2 * X

VMEM = pl.BlockSpec(memory_space=pltpu.VMEM)
HBM = pl.BlockSpec(memory_space=pltpu.HBM)
ANY = pl.BlockSpec(memory_space=pl.ANY)


def dot(a, b, ca, cb):
    return lax.dot_general(a, b, (((ca,), (cb,)), ((), ())), preferred_element_type=F32)


def call(kernel, outs, args, flops, after=(), ins=VMEM, out=VMEM, scratch=(), vmem=16):
    nbytes = sum(a.size * a.dtype.itemsize for a in args)
    nbytes += sum(o.size * o.dtype.itemsize for o in outs)

    ins = ins if isinstance(ins, list) else [ins] * len(args)
    out = out if isinstance(out, list) else [out] * len(outs)

    def body(*refs):
        kernel(*refs[: len(args)], *refs[len(args) + len(after) :])

    return pl.pallas_call(
        body,
        out_shape=outs,
        in_specs=ins + [ANY] * len(after),
        out_specs=out,
        scratch_shapes=list(scratch),
        compiler_params=pltpu.CompilerParams(vmem_limit_bytes=vmem << 20),
        cost_estimate=pl.CostEstimate(flops=flops, bytes_accessed=nbytes, transcendentals=0),
    )(*args, *after)


def array(shape, dtype):
    return jax.ShapeDtypeStruct(shape, dtype)


def at(h):
    return slice(h * HEAD_DIM, (h + 1) * HEAD_DIM)


def my_core():
    return lax.rem(lax.axis_index("ctx"), CORES)


def shift(i):
    return i // (2 * X * CORES)


def my_half():
    i = lax.axis_index("ctx")
    return lax.rem(i % CORES + shift(i), 2)


OWN, OTHER = 0, 1
FIRST = ((0, 1), (1, 3))


def cols(side, j, half):
    mine = my_half()
    base = (mine if side == OWN else 1 - mine) * (half * HEAD_DIM)
    return pl.ds(pl.multiple_of(base + j * HEAD_DIM, HEAD_DIM), HEAD_DIM)


def state_own_kernel(side, a_ref, b_ref, s_ref):
    half = s_ref.shape[0] // HEAD_DIM
    for j in range(half):
        c = cols(side, j, half)
        s_ref[at(j), :] = dot(a_ref[:, c], b_ref[:, c], 0, 0)


def columns(side, half):
    mine = my_half()
    base = (mine if side == OWN else 1 - mine) * (half * HEAD_DIM)
    return pl.ds(pl.multiple_of(base, half * HEAD_DIM), half * HEAD_DIM)


def state_kernel(side, a_hbm, b_hbm, a_ref, b_ref, s_ref, sems):
    half = s_ref.shape[0] // HEAD_DIM
    copies = []
    for i, which in enumerate((side, OWN + OTHER - side)):
        c = columns(which, half)
        for j, (src, dst) in enumerate(((a_hbm, a_ref), (b_hbm, b_ref))):
            copies.append(pltpu.make_async_copy(src.at[:, c], dst.at[:, c], sems.at[i, j]))
            copies[-1].start()
    for copy in copies[:2]:
        copy.wait()
    state_own_kernel(side, a_ref, b_ref, s_ref)
    for copy in copies[2:]:
        copy.wait()


def triangle(n, flip=False):
    rows = lax.broadcasted_iota(jnp.int32, (n, n), 0)
    cols = lax.broadcasted_iota(jnp.int32, (n, n), 1)
    return rows <= cols if flip else cols <= rows


def lower(a, b):
    n = a.shape[0] // 2
    keep = triangle(n)
    top = jnp.where(keep, dot(a[:n], b[:n], 1, 1), 0.0).astype(BF)
    left = dot(a[n:], b[:n], 1, 1).astype(BF)
    right = jnp.where(keep, dot(a[n:], b[n:], 1, 1), 0.0).astype(BF)
    return top, left, right


def lower_t(a, b):
    n = a.shape[0] // 2
    keep = triangle(n, True)
    top = jnp.where(keep, dot(b[:n], a[:n], 1, 1), 0.0).astype(BF)
    left = dot(b[:n], a[n:], 1, 1).astype(BF)
    right = jnp.where(keep, dot(b[n:], a[n:], 1, 1), 0.0).astype(BF)
    return top, left, right


def intra_kernel(side, q_ref, k_ref, v_ref, qt_ref, o_ref):
    n = q_ref.shape[0] // 2
    half = o_ref.shape[1] // HEAD_DIM
    for j in range(half):
        c = cols(side, j, half)
        q, k, v = q_ref[:, c], k_ref[:, c], v_ref[:, c]
        qt_ref[at(j), :] = q.T
        top, left, right = lower(q, k)
        o_ref[:n, at(j)] = dot(top, v[:n], 1, 0)
        o_ref[n:, at(j)] = dot(left, v[:n], 1, 0) + dot(right, v[n:], 1, 0)


def weights_kernel(q_ref, k_ref, own_ref, other_ref):
    half = own_ref.shape[0] // 3
    for side, wt_ref in ((OWN, own_ref), (OTHER, other_ref)):
        for j in range(half):
            c = cols(side, j, half)
            for i, block in enumerate(lower_t(q_ref[:, c], k_ref[:, c])):
                wt_ref[3 * j + i] = block


def mix_kernel(side, q_ref, s_ref, i_ref, c_ref, g_ref, *refs):
    before_ref = refs[0] if side == OTHER else None
    m_ref, p_ref = refs[-2:]
    half = m_ref.shape[1] // HEAD_DIM
    state = [s_ref[at(j), :].astype(BF) for j in range(half)]
    for i in range(q_ref.shape[0] // 128):
        rows = slice(i * 128, (i + 1) * 128)
        squares = jnp.zeros((128, HEAD_DIM), F32)
        products = jnp.zeros((128, HEAD_DIM), F32)
        for j in range(half):
            c = cols(side, j, half)
            m = i_ref[rows, at(j)] + dot(q_ref[rows, c], state[j], 1, 0)
            m_ref[rows, at(j)] = m
            squares = squares + m * m
            products = products + (c_ref[rows, c].astype(F32) * g_ref[:, c]) * m
        for row, value in ((i, squares), (4 + i, products)):
            value = jnp.sum(value.T, axis=0, keepdims=True)
            if side == OTHER:
                value = value + before_ref[row : row + 1, :]
            p_ref[row : row + 1, :] = value


def spread(row):
    return jnp.broadcast_to(row, (128, 128)).T


def grad(side, qt_ref, m_ref, c_ref, g_ref, inv_ref, cf_ref, gm_ref, s_ref):
    half = m_ref.shape[1] // HEAD_DIM
    for j in range(half):
        c = cols(side, j, half)
        scaled = c_ref[:, c].astype(F32) * g_ref[:, c]
        gm = (inv_ref[...] * scaled - m_ref[:, at(j)] * cf_ref[...]).astype(BF)
        gm_ref[:, at(j)] = gm
        s_ref[at(j), :] = dot(qt_ref[at(j), :], gm, 1, 0)


def grad_other_kernel(qt_ref, m_ref, c_ref, g_ref, p0, p1, p2, p3, gm_ref, s_ref, inv_ref, cf_ref):
    width = HEADS * HEAD_DIM
    sums = p0[...] + p1[...] + p2[...] + p3[...]
    inverse = lax.rsqrt(sums[:4] / width + EPSILON)
    coef = inverse * inverse * inverse * sums[4:] / width
    for i in range(4):
        rows = slice(i * 128, (i + 1) * 128)
        inv_ref[rows, :] = spread(inverse[i : i + 1])
        cf_ref[rows, :] = spread(coef[i : i + 1])
    grad(OTHER, qt_ref, m_ref, c_ref, g_ref, inv_ref, cf_ref, gm_ref, s_ref)


def grad_own_kernel(qt_ref, m_ref, c_ref, g_ref, inv_ref, cf_ref, gm_ref, s_ref):
    grad(OWN, qt_ref, m_ref, c_ref, g_ref, inv_ref, cf_ref, gm_ref, s_ref)


def back(
    side, heads, q_ref, k_ref, v_ref, gm_ref, s_ref, m_ref, inv_ref, g_ref, wt_ref,
    at_ref, gq_ref, gk_ref, gv_ref, then=lambda j: None,
):
    n = q_ref.shape[0] // 2
    half = gm_ref.shape[1] // HEAD_DIM
    for i, j in enumerate(heads):
        c = cols(side, j, half)
        at_ref[:, at(i)] = (m_ref[:, at(j)] * inv_ref[...] * g_ref[:, c]).astype(BF)
        q, k, v, gm = q_ref[:, c], k_ref[:, c], v_ref[:, c], gm_ref[:, at(j)]
        top, left, right = lower(gm, v)
        s = s_ref[at(j), :].astype(BF)
        gq_ref[:n, at(i)] = (dot(top, k[:n], 1, 0) + dot(gm[:n], s, 1, 1)).astype(BF)
        gq_ref[n:, at(i)] = (
            dot(left, k[:n], 1, 0) + dot(right, k[n:], 1, 0) + dot(gm[n:], s, 1, 1)
        ).astype(BF)
        gk_ref[:n, at(i)] = dot(top, q[:n], 0, 0) + dot(left, q[n:], 0, 0)
        gk_ref[n:, at(i)] = dot(right, q[n:], 0, 0)
        top, left, right = wt_ref[3 * j], wt_ref[3 * j + 1], wt_ref[3 * j + 2]
        gv_ref[:n, at(i)] = dot(top, gm[:n], 1, 0) + dot(left, gm[n:], 1, 0)
        gv_ref[n:, at(i)] = dot(right, gm[n:], 1, 0)
        then(j)


def send_out(pairs, half, sems):
    copies = []
    for i, (side, src, dst) in enumerate(pairs):
        copies.append(pltpu.make_async_copy(src, dst.at[:, columns(side, half)], sems.at[i]))
        copies[-1].start()
    return copies


def send_two(j, half, pairs, sems):
    copies = []
    if j % 2:
        base = cols(OTHER, j - 1, half).start
        c = pl.ds(pl.multiple_of(base, 2 * HEAD_DIM), 2 * HEAD_DIM)
        here = slice((j - 1) * HEAD_DIM, (j + 1) * HEAD_DIM)
        for i, (src, dst) in enumerate(pairs):
            copies.append(pltpu.make_async_copy(src.at[:, here], dst.at[:, c], sems.at[i, j]))
            copies[-1].start()
    return copies


def send_heads(j, half, side, pairs, sems):
    copies = []
    for i, (src, dst) in enumerate(pairs):
        copies.append(
            pltpu.make_async_copy(src.at[:, at(j)], dst.at[:, cols(side, j, half)], sems.at[i, j])
        )
        copies[-1].start()
    return copies


def back_other_kernel(heads, *refs):
    back(OTHER, heads, *refs)


def back_own_kernel(*refs):
    ins, others = refs[:9], refs[9:13]
    gk_ref, gv_ref, at_hbm, gq_hbm, at_ref, gq_ref, sems, head_sems = refs[13:]
    half = gk_ref.shape[1] // HEAD_DIM
    copies = []
    for i, src in enumerate(others):
        first, count = FIRST[i // 2]
        base = cols(OTHER, first, half).start
        dst = (at_hbm, gq_hbm)[i % 2].at[:, pl.ds(pl.multiple_of(base, HEAD_DIM), count * HEAD_DIM)]
        copies.append(pltpu.make_async_copy(src, dst, sems.at[i]))
        copies[-1].start()
    pairs = ((at_ref, at_hbm), (gq_ref, gq_hbm))

    def then(j):
        copies.extend(send_heads(j, half, OWN, pairs, head_sems))

    back(OWN, range(half), *ins, at_ref, gq_ref, gk_ref, gv_ref, then)
    for copy in copies:
        copy.wait()


def last(side, k_ref, v_ref, s_ref, inner, gk_ref, gv_ref, then=lambda j: None):
    half = gk_ref.shape[1] // HEAD_DIM
    pieces = [(*refs, i) for refs in inner for i in range(refs[0].shape[1] // HEAD_DIM)]
    for j, (gki_ref, gvi_ref, i) in enumerate(pieces):
        c = cols(side, j, half)
        s = s_ref[at(j), :].astype(BF)
        gk_ref[:, at(j)] = (gki_ref[:, at(i)] + dot(v_ref[:, c], s, 1, 1)).astype(BF)
        gv_ref[:, at(j)] = (gvi_ref[:, at(i)] + dot(k_ref[:, c], s, 1, 0)).astype(BF)
        then(j)


def last_own_kernel(k_ref, v_ref, s_ref, gki_ref, gvi_ref, gk_ref, gv_ref):
    last(OWN, k_ref, v_ref, s_ref, ((gki_ref, gvi_ref),), gk_ref, gv_ref)


def last_other_kernel(
    k_ref, v_ref, s_ref, gka_ref, gva_ref, gkb_ref, gvb_ref, gko_ref, gvo_ref,
    gk_hbm, gv_hbm, gk_ref, gv_ref, sems, head_sems,
):
    half = gk_ref.shape[1] // HEAD_DIM
    inner = ((gka_ref, gva_ref), (gkb_ref, gvb_ref))
    copies = send_out([(OWN, gko_ref, gk_hbm), (OWN, gvo_ref, gv_hbm)], half, sems)
    pairs = ((gk_ref, gk_hbm), (gv_ref, gv_hbm))

    def then(j):
        copies.extend(send_two(j, half, pairs, head_sems))

    last(OTHER, k_ref, v_ref, s_ref, inner, gk_ref, gv_ref, then)
    for copy in copies:
        copy.wait()


def add_kernel(a_ref, b_ref, o_ref):
    o_ref[...] = (a_ref[...] + b_ref[...]).reshape(o_ref.shape)


def finish_kernel(reverse, g_ref, keep_ref, other_ref, mine_ref, give_ref):
    first = g_ref[...].reshape(keep_ref.shape)
    leads = my_core() == (1 if reverse else 0)
    second = first + jnp.where(leads, keep_ref[...], other_ref[...])
    mine_ref[...] = jnp.where(leads, first, second)
    give_ref[...] = jnp.where(leads, second, first)


def running_kernel(reverse, g_ref, o_ref, t_ref):
    total = jnp.zeros(g_ref.shape[1:], F32)
    for i in range(g_ref.shape[0]) if not reverse else reversed(range(g_ref.shape[0])):
        o_ref[i] = total
        total = total + g_ref[i]
    t_ref[...] = total


def rank(reverse):
    pair = lax.axis_index("ctx") // (2 * X * CORES)
    return 3 - pair if reverse else pair


def middle_kernel(reverse, t_ref, far_ref, o_ref):
    place = rank(reverse)
    own = jnp.where(place == 3, 0.0, t_ref[...])
    o_ref[...] = own + jnp.where(place >= 2, far_ref[...], 0.0)


def outer_kernel(reverse, g_ref, far_ref, near_ref, o_ref):
    place = rank(reverse)
    total = jnp.where(place >= 2, far_ref[...], 0.0) + jnp.where(place >= 1, near_ref[...], 0.0)
    for i in range(g_ref.shape[0]):
        o_ref[i] = g_ref[i] + total


def carried(send, reverse, windows):
    count = lax.axis_size("ctx")
    pieces_of = (PAIR, send.shape[0] // PAIR, HEAD_DIM)
    swap = [(i, i ^ 1) for i in range(count)]
    def on(chip, half):
        return chip * CORES + (half + shift(chip * CORES)) % CORES

    groups = [
        [on(pair * PAIR + i, half) for i in range(PAIR)]
        for pair in range(count // (PAIR * CORES))
        for half in range(2)
    ]
    across = (6, 7, 4, 5, 2, 3, 0, 1)

    def partners(of):
        chips = [(z * X + x, of(z) * X + x) for z in range(len(across)) for x in range(X)]
        return [(on(a, half), on(b, half)) for a, b in chips for half in range(2)]

    near_z = partners(lambda z: z ^ 2)
    far_z = partners(lambda z: across[z])

    def add(a, b, after, shape):
        return call(add_kernel, [array(shape, F32)], [a, b], a.size, after, vmem=4)[0]

    other = lax.ppermute(send, "ctx", swap)
    keep = windows[0](send)[-1]
    pieces = add(keep, other, (), pieces_of)
    pieces = lax.all_to_all(pieces, "ctx", 0, 0, axis_index_groups=groups)
    inner, total = call(
        functools.partial(running_kernel, reverse),
        [array(pieces.shape, F32), array(pieces.shape[1:], F32)],
        [pieces],
        pieces.size,
        vmem=4,
    )
    far = lax.ppermute(total, "ctx", far_z)
    after = windows[1](total)[-1:]
    (total,) = call(
        functools.partial(middle_kernel, reverse),
        [array(total.shape, F32)],
        [total, far],
        total.size,
        after,
        vmem=4,
    )
    near = lax.ppermute(total, "ctx", near_z)
    after = windows[2](total)[-1:]
    (pieces,) = call(
        functools.partial(outer_kernel, reverse),
        [array(pieces.shape, F32)],
        [inner, far, near],
        pieces.size,
        after,
        vmem=4,
    )
    pieces = lax.all_to_all(pieces, "ctx", 0, 0, axis_index_groups=groups)
    mine, give = call(
        functools.partial(finish_kernel, reverse),
        [array(send.shape, F32)] * 2,
        [pieces, keep, other],
        pieces.size,
        vmem=4,
    )
    theirs = lax.ppermute(give, "ctx", swap)
    windows[3](give, mine)
    return mine, theirs


def body(query, keys, values, gain, cotangent):
    length, width = query.shape
    half = width // HEAD_DIM // 2
    square = 2 * length * length * HEAD_DIM * half
    small = 2 * length * HEAD_DIM * HEAD_DIM * half
    gain = gain.reshape(1, width)
    whole = array((length, width), BF)
    part = lambda dtype: array((length, half * HEAD_DIM), dtype)
    states = array((half * HEAD_DIM, HEAD_DIM), F32)
    lanes = array((length, HEAD_DIM), F32)
    rows = array((8, 128), F32)
    dmas = pltpu.SemaphoreType.DMA
    halves = [pltpu.VMEM((length, half * HEAD_DIM), BF)] * 2
    made = {}

    def made_by(name, side, kernel, outs, args, flops, after=(), **options):
        made[name, side] = call(functools.partial(kernel, side), outs, args, flops, after, **options)
        return made[name, side]

    in_hbm = [pltpu.with_memory_space_constraint(a, pltpu.HBM) for a in (keys, values)]

    keys, values, send = made_by(
        "state", OTHER, state_kernel, [whole, whole, states], in_hbm, small,
        ins=HBM, scratch=[dmas((2, 2))],
    )

    def state_own(ready):
        return made_by("state", OWN, state_own_kernel, [states], [keys, values], small, [ready])

    def intra(side, ready):
        outs = [
            array((half * HEAD_DIM, length), BF),
            part(F32),
        ]
        args = [query, keys, values]
        return made_by("intra", side, intra_kernel, outs, args, 3 * square, [ready])

    def mix(side, before, after, *sums):
        args = [query, before, made["intra", side][1], cotangent, gain, *sums]
        return made_by("mix", side, mix_kernel, [part(F32), rows], args, small, after)

    mine, theirs = carried(
        send,
        False,
        [
            state_own,
            lambda ready: intra(OWN, ready),
            lambda ready: intra(OTHER, ready),
            lambda ready, mine: mix(OWN, mine, [ready]),
        ],
    )
    before = (mine, theirs)
    _, sums = mix(OTHER, theirs, (), made["mix", OWN][1])
    heads = lax.axis_size("head")
    places = range(lax.axis_size("ctx"))

    def turn(first, second):
        by = (first, second)
        return [
            (i * heads + j, i * heads + (j ^ by[i % CORES])) for i in places for j in range(heads)
        ]

    others = [
        lax.ppermute(sums, ("ctx", "head"), turn(*by)) for by in zip((1, 3, 2), (3, 2, 1))
    ]

    weights_t = call(
        weights_kernel,
        [array((3 * half, length // 2, length // 2), BF)] * 2,
        [query, keys],
        2 * square,
        [sums],
    )

    def grad_args(side):
        return [made["intra", side][0], made["mix", side][0], cotangent, gain]

    gm_other, send, inverse, coef = call(
        grad_other_kernel,
        [part(BF), states, lanes, lanes],
        grad_args(OTHER) + [sums, *others],
        small,
        weights_t[:1],
    )

    def grad_own(ready):
        made["grad"] = call(
            grad_own_kernel,
            [part(BF), states],
            grad_args(OWN) + [inverse, coef],
            small,
            [ready],
        )
        return made["grad"]

    def back_args(side):
        gm = gm_other if side == OTHER else made["grad"][0]
        mixture, weights = made["mix", side][0], weights_t[side]
        return [query, keys, values, gm, before[side], mixture, inverse, gain, weights]

    made["back"] = []

    def back_other(ready):
        first, count = FIRST[len(made["back"])]
        piece = lambda dtype: array((length, count * HEAD_DIM), dtype)
        made["back"].append(
            call(
                functools.partial(back_other_kernel, range(first, first + count)),
                [piece(BF), piece(BF), piece(F32), piece(F32)],
                back_args(OTHER),
                square * count,
                [ready],
            )
        )
        return made["back"][-1]

    def grad_and_back(ready):
        back_piece = back_other(ready)
        return [*back_piece, *grad_own(back_piece[-1])]

    def back_own(ready):
        *made["rows"], gk, gv = call(
            lambda *refs: back_own_kernel(*refs[:13], *refs[15:17], *refs[13:15], *refs[17:]),
            [whole, whole, part(F32), part(F32)],
            [*back_args(OWN), *made["back"][0][:2], *made["back"][1][:2]],
            4 * square,
            [ready],
            out=[HBM, HBM, VMEM, VMEM],
            scratch=halves + [dmas((4,)), dmas((2, half))],
        )
        made["own"] = [gk, gv]
        return made["own"]

    def last_own(ready, mine):
        args = [keys, values, mine, *made["own"]]
        made["last"] = call(last_own_kernel, [part(BF), part(BF)], args, 2 * small, [ready])
        return made["last"]

    _, theirs = carried(send, True, [grad_and_back, back_other, back_own, last_own])
    grads = call(
        last_other_kernel,
        [whole, whole],
        [keys, values, theirs, *made["back"][0][2:], *made["back"][1][2:], *made["last"]],
        2 * small,
        out=HBM,
        scratch=halves + [dmas((2,)), dmas((2, half))],
    )
    return (*made["rows"], *grads)


def solution(mesh):
    spec = P("ctx", "head")
    return jax.shard_map(
        body,
        mesh=mesh,
        in_specs=(spec, spec, spec, P("head"), spec),
        out_specs=(spec,) * 4,
        check_vma=False,
    )
```
